512 devices in a mesh: aux: 8 (over x, z_lo), row: 64 (over z_hi, y, core).
Axes of the slice: x: 4, y: 8, z: 8 (z_hi: 4, z_lo: 2; z = z_hi * 2 + z_lo), core: 2. Of those that a mesh axis runs over, the one named last changes fastest.
Arguments:
- three_center: bfloat16 [32, 64, 1024, 384], P('aux', 'row'), may hold values from -0.3125 to 0.3125
- pattern: int32 [32, 64, 6], P('aux', 'row'), may hold values from 0 to 63, as said below
- live_count: int32 [32, 64], P('aux', 'row'), may hold values from 1 to 6, as said below
- density_factor: bfloat16 [4096, 512], P('row'), may hold values from -6 to 6
- screen: int32 [64, 4], P('row'), may hold values 0 or 1
Outputs:
- exchange: float32 [4096, 64], P('row')
The draws below stay inside these ranges and needn't reach their ends.
Inputs may be any that keep to these rules, and one draw needn't show every extreme that they name: `pattern`: the 6 slots of one auxiliary block and atom block name distinct atom blocks. `live_count`: in every auxiliary block some atom block has all 6 slots live.
All inputs are finite; a program needn't handle non-finite values. No bound on the sum of `screen` on one device may be relied on, other than what follows from the above.
Results may differ from the reference program's by a relative error of at most 0.0038.
Values may be sent and summed in bfloat16 or wider, within the bound.
No kernel may reach another device: no remote copies, remote signals or barrier semaphores. Data moves between devices by JAX's collectives and lax.ppermute only.
A program may use at most 64 MiB of HBM per device.

```python
import math
import jax
import jax.numpy as jnp
from jax import lax

BS = 64
AB = 16
KNZ = 6
OBS = 128
NOCC = 512
NB = 64
NBASIS = 4096
NAB = 32
NAUX = 512


def draw_pattern(key, part):
    key = jax.random.fold_in(key, 11)
    scores = jax.random.randint(key, (NAB, NB, NB), 0, 2 ** 20) * NB + jnp.arange(NB, dtype=jnp.int32)
    ranking = jnp.argsort(scores, axis=-1, stable=True)
    return ranking[:, :, :KNZ].astype(jnp.int32)


def draw_live_count(key, part):
    key = jax.random.fold_in(key, 23)
    count_key, place_key = jax.random.split(key)
    counts = jax.random.randint(count_key, (NAB, NB), 1, KNZ + 1)
    fullest = jax.random.randint(place_key, (NAB, 1), 0, NB)
    return jnp.where(jnp.arange(NB)[None, :] == fullest, KNZ, counts).astype(jnp.int32)


def plant(result, rng, smallest, largest):
    dims = result.shape
    spot = [jax.random.randint(jax.random.fold_in(rng, axis), (), 0, dims[axis]) for axis in range(len(dims))]
    result = result.at[tuple(spot)].set(smallest)
    longest = dims.index(max(dims))
    spot[longest] = (spot[longest] + 1) % dims[longest]
    return result.at[tuple(spot)].set(largest)


def levels(key, extent, shards, low, largest):
    gain = 1.0
    for position, shards_of in shards:
        steps = jax.random.uniform(jax.random.fold_in(jax.random.fold_in(key, 6), position), (shards_of,), jnp.float32, low / len(shards), largest / len(shards))
        gain = gain * jnp.repeat(jnp.exp(steps), extent[position] // shards_of).reshape((-1,) + (1,) * (len(extent) - 1 - position))
    return gain


def bell_draw(own_key, dims, deviation, most, cuts=(), held_as=jnp.bfloat16):
    level = levels(own_key, dims, cuts, -0.22, 0.18) if cuts else 1.0
    array = jax.random.normal(own_key, dims, jnp.float32) * deviation * level
    return jnp.minimum(jnp.maximum(array, -most), most).astype(held_as)


def setup_inputs(seed: int = 0) -> dict:
    key_of = jax.random.split(jax.random.key(seed), 6)
    return {
        "three_center": bell_draw(key_of[0], (NAB, NB, AB * BS, KNZ * BS), (KNZ * BS) ** -0.5, 0.3125, ((0, 8), (1, 64))),
        "pattern": draw_pattern(jax.random.fold_in(key_of[5], 71), 0),
        "live_count": draw_live_count(jax.random.fold_in(key_of[5], 71), 0),
        "density_factor": bell_draw(key_of[3], (NBASIS, NOCC), 1.0, 6.0, ((0, 64),)),
        "screen": plant((jax.random.randint(key_of[4], (NB, NOCC // OBS), 0, 4) < 3).astype(jnp.int32), jax.random.fold_in(key_of[4], 1), 0, 1),
    }


def reference(three_center, pattern, live_count, density_factor, screen):
    screen_mask = jnp.repeat(jnp.repeat(screen, OBS, axis=1), BS, axis=0).astype(jnp.float32)
    screened = density_factor.astype(jnp.float32) * screen_mask
    blocks = screened.reshape(NB, BS, NOCC)
    slot_ids = jnp.arange(KNZ, dtype=jnp.int32)
    partner = (jnp.arange(NB, dtype=jnp.int32) + NB // 2) % NB

    def aux_step(running, inputs):
        tensor, places, counts = inputs
        gathered = blocks[places]
        alive_mask = (slot_ids[None, :] < counts[:, None]).astype(jnp.float32)
        gathered = gathered * alive_mask[:, :, None, None]
        gathered = gathered.reshape(NB, KNZ * BS, NOCC)
        half_done = jnp.einsum('rpk,rkn->rpn', tensor.astype(jnp.float32), gathered)
        half_done = lax.optimization_barrier(half_done.astype(jnp.bfloat16)).astype(jnp.float32)
        half_done = half_done.reshape(NB, AB, BS, NOCC)
        running = running + jnp.einsum('rpmi,rpni->rmn', half_done, half_done[partner])
        return (running, None)
    initial = jnp.zeros((NB, BS, BS), jnp.float32)
    running, unused = lax.scan(aux_step, initial, (three_center, pattern, live_count))
    scaling = 1.0 / math.sqrt(NAUX * NOCC)
    return (-scaling * running).reshape(NB * BS, BS).astype(jnp.float32)
```

```python
import math

import jax
import jax.numpy as jnp
from jax import lax
from jax.experimental import pallas as pl
from jax.experimental.pallas import tpu as pltpu
from jax.sharding import Mesh, PartitionSpec as P

BS = 64
AB = 16
KNZ = 6
OBS = 128
NOCC = 512
ROWS = AB * BS
COLS = KNZ * BS
TILE = 256
AUX = ("x", "zl")
ROW = ("zp", "zm", "y", "c")
SWAP = [(0, 1), (1, 0)]


def gather_slots(whole_ref, gathered_ref, pattern_ref, count_ref, base):
    for slot in range(KNZ):
        rows = pl.ds(slot * BS, BS)
        block = pattern_ref[base * KNZ + slot]
        start = pl.multiple_of(block * BS, BS)
        alive = slot < count_ref[base]

        @pl.when(alive)
        def _():
            gathered_ref[rows, :] = whole_ref[pl.ds(start, BS), :]

        @pl.when(jnp.logical_not(alive))
        def _():
            gathered_ref[rows, :] = jnp.zeros((BS, NOCC), jnp.bfloat16)


def own_kernel(side, pattern, count, their_pattern, their_count, tensor, whole, half, their_gathered, gathered):
    position = side[0] * 2 + pl.program_id(0)
    gather_slots(whole, gathered, pattern, count, position)
    gather_slots(whole, their_gathered.at[0], their_pattern, their_count, position)

    def step(index, carry):
        rows = pl.ds(pl.multiple_of(index * TILE, TILE), TILE)
        product = jnp.dot(tensor[0, rows, :], gathered[...], preferred_element_type=jnp.float32)
        half[0, rows, :] = product.astype(jnp.bfloat16)
        return carry

    lax.fori_loop(0, ROWS // TILE, step, 0)


def own_part(side, pattern, count, their_pattern, their_count, tensor, whole):
    spec = pltpu.PrefetchScalarGridSpec(
        num_scalar_prefetch=5,
        grid=(2,),
        in_specs=[
            pl.BlockSpec((1, ROWS, COLS), lambda j, side, *_: (side[0] * 2 + j, 0, 0)),
            pl.BlockSpec(whole.shape, lambda j, *_: (0, 0)),
        ],
        out_specs=[
            pl.BlockSpec((1, ROWS, NOCC), lambda j, *_: (j, 0, 0)),
            pl.BlockSpec((1, COLS, NOCC), lambda j, *_: (j, 0, 0)),
        ],
        scratch_shapes=[pltpu.VMEM((COLS, NOCC), jnp.bfloat16)],
    )
    return pl.pallas_call(
        own_kernel,
        grid_spec=spec,
        out_shape=[
            jax.ShapeDtypeStruct((2, ROWS, NOCC), jnp.bfloat16),
            jax.ShapeDtypeStruct((2, COLS, NOCC), jnp.bfloat16),
        ],
        compiler_params=pltpu.CompilerParams(vmem_limit_bytes=32 * 2**20),
        cost_estimate=pl.CostEstimate(
            flops=4 * ROWS * COLS * NOCC, bytes_accessed=9 * 2**20, transcendentals=0
        ),
        name="own_half",
    )(side, pattern, count, their_pattern, their_count, tensor, whole)


def pair_kernel(tensor, gathered, own_half, out, total):
    step_id = pl.program_id(0)

    @pl.when(step_id == 0)
    def _():
        total[...] = jnp.zeros_like(total)

    def step(index, carry):
        rows = pl.ds(pl.multiple_of(index * TILE, TILE), TILE)
        product = jnp.dot(tensor[0, rows, :], gathered[0], preferred_element_type=jnp.float32)
        their_half = product.astype(jnp.bfloat16)
        total[...] += lax.dot_general(
            own_half[0, rows, :], their_half, (((1,), (1,)), ((), ())), preferred_element_type=jnp.float32
        )
        return carry

    lax.fori_loop(0, ROWS // TILE, step, 0)

    @pl.when(step_id == pl.num_programs(0) - 1)
    def _():
        tile = total[0:BS, 0:BS]
        for block in range(1, TILE // BS):
            rows = slice(block * BS, (block + 1) * BS)
            tile += total[rows, rows]
        out[...] = tile


def pair_part(their_tensor, their_gathered, own_half):
    return pl.pallas_call(
        pair_kernel,
        grid=(2,),
        in_specs=[
            pl.BlockSpec((1, ROWS, COLS), lambda j: (j, 0, 0)),
            pl.BlockSpec((1, COLS, NOCC), lambda j: (j, 0, 0)),
            pl.BlockSpec((1, ROWS, NOCC), lambda j: (j, 0, 0)),
        ],
        out_specs=pl.BlockSpec((BS, BS), lambda j: (0, 0)),
        out_shape=jax.ShapeDtypeStruct((BS, BS), jnp.float32),
        scratch_shapes=[pltpu.VMEM((TILE, TILE), jnp.float32)],
        compiler_params=pltpu.CompilerParams(vmem_limit_bytes=32 * 2**20),
        cost_estimate=pl.CostEstimate(
            flops=6 * ROWS * COLS * NOCC, bytes_accessed=5 * 2**20, transcendentals=0
        ),
        name="pair_tile",
    )(their_tensor, their_gathered, own_half)


def per_device(three_center, pattern, live_count, density_factor, screen):
    side = lax.axis_index("zp")
    tensor = three_center.reshape(4, ROWS, COLS)
    sent = lax.dynamic_slice_in_dim(tensor, (1 - side) * 2, 2, 0)
    their_tensor = lax.ppermute(sent, "zp", SWAP)

    screen_mask = jnp.repeat(screen, OBS, axis=1).astype(jnp.bfloat16)
    screened = density_factor * screen_mask
    column = lax.all_gather(screened, ("zp", "zm"))
    plane = lax.all_gather(lax.optimization_barrier(column), ("y", "c"))
    whole = plane.transpose(1, 0, 2, 3).reshape(-1, NOCC)

    numbers = jnp.concatenate([pattern.reshape(-1), live_count.reshape(-1)])
    their_numbers = lax.ppermute(numbers, "zp", SWAP)
    split = 4 * KNZ
    own_half, their_gathered = own_part(
        side.reshape(1), numbers[:split], numbers[split:], their_numbers[:split], their_numbers[split:], tensor, whole
    )
    tile = pair_part(their_tensor, their_gathered, own_half)

    group = ("x", "zl", "zp")
    spread = jnp.broadcast_to(tile[None], (16, BS, BS))
    tiles = lax.all_to_all(spread, group, 0, 0, tiled=True)
    tiles = tiles.reshape(8, 2, BS, BS).sum(axis=0)
    mine = lax.dynamic_index_in_dim(tiles, side, 0, keepdims=False)
    other = lax.dynamic_index_in_dim(tiles, 1 - side, 0, keepdims=False)
    functions = 32 * AB * NOCC
    return (mine + other.T) * (-1.0 / math.sqrt(functions))


def solution(mesh):
    parts = Mesh(mesh.devices.reshape(4, 2, 2, 2, 8, 2), ("x", "zl", "zp", "zm", "y", "c"))
    placed = (
        P(AUX, ROW, None, None),
        P(AUX, ROW, None),
        P(AUX, ROW),
        P(ROW, None),
        P(ROW, None),
    )
    return jax.shard_map(
        per_device, mesh=parts, in_specs=placed, out_specs=P(ROW, None), check_vma=False
    )
```

```python
import math

import jax
import jax.numpy as jnp
from jax import lax
from jax.experimental import pallas as pl
from jax.experimental.pallas import tpu as pltpu
from jax.sharding import Mesh, PartitionSpec as P

BS = 64
AB = 16
KNZ = 6
OBS = 128
NOCC = 512
ROWS = AB * BS
COLS = KNZ * BS
TILE = 256
AUX = ("x", "zl")
ROW = ("zp", "zm", "y", "c")
SWAP = [(0, 1), (1, 0)]
COLUMN = 4 * BS
PLANE = 8 * COLUMN
HEADER = 16
STARTS = (0, 2048)
VMEM_BYTES = 40 * 2**20


def vmem_params():
    return pltpu.CompilerParams(vmem_limit_bytes=VMEM_BYTES)


def in_vmem(count):
    return [pl.BlockSpec(memory_space=pltpu.VMEM)] * count


def gather_slots(whole, gathered, place, count, position):
    for slot in range(KNZ):
        rows = pl.ds(slot * BS, BS)
        start = pl.multiple_of(place[position * KNZ + slot], BS)
        alive = slot < count[position]

        @pl.when(alive)
        def _():
            gathered[rows, :] = whole[pl.ds(start, BS), :]

        @pl.when(jnp.logical_not(alive))
        def _():
            gathered[rows, :] = jnp.zeros((BS, NOCC), jnp.bfloat16)


def own_kernel(side, place, count, their_place, their_count, tensor, *refs):
    pieces = refs[:-5]
    half, their_gathered, gathered, whole, sem = refs[-5:]

    @pl.when(pl.program_id(0) == 0)
    def _():
        copies = []
        for core, piece in enumerate(pieces):
            for block in range(NOCC // OBS):
                rows, columns = pl.ds(core * PLANE, PLANE), pl.ds(block * OBS, OBS)
                source = piece.at[pl.ds(block * PLANE, PLANE), :]
                copy = pltpu.make_async_copy(source, whole.at[rows, columns], sem.at[core * 4 + block])
                copy.start()
                copies.append(copy)
        for copy in copies:
            copy.wait()

    position = side[0] * 2 + pl.program_id(0)
    gather_slots(whole, gathered, place, count, position)
    gather_slots(whole, their_gathered.at[0], their_place, their_count, position)

    def step(index, carry):
        rows = pl.ds(pl.multiple_of(index * TILE, TILE), TILE)
        product = jnp.dot(tensor[0, rows, :], gathered[...], preferred_element_type=jnp.float32)
        half[0, rows, :] = product.astype(jnp.bfloat16)
        return carry

    lax.fori_loop(0, ROWS // TILE, step, 0)


def own_part(side, place, count, their_place, their_count, tensor, pieces):
    spec = pltpu.PrefetchScalarGridSpec(
        num_scalar_prefetch=5,
        grid=(2,),
        in_specs=[pl.BlockSpec((1, ROWS, COLS), lambda j, side, *_: (side[0] * 2 + j, 0, 0))]
        + [pl.BlockSpec(memory_space=pl.ANY)] * len(pieces),
        out_specs=[
            pl.BlockSpec((1, ROWS, NOCC), lambda j, *_: (j, 0, 0)),
            pl.BlockSpec((1, COLS, NOCC), lambda j, *_: (j, 0, 0)),
        ],
        scratch_shapes=[
            pltpu.VMEM((COLS, NOCC), jnp.bfloat16),
            pltpu.VMEM((64 * BS, NOCC), jnp.bfloat16),
            pltpu.SemaphoreType.DMA((8,)),
        ],
    )
    return pl.pallas_call(
        own_kernel,
        grid_spec=spec,
        out_shape=[
            jax.ShapeDtypeStruct((2, ROWS, NOCC), jnp.bfloat16),
            jax.ShapeDtypeStruct((2, COLS, NOCC), jnp.bfloat16),
        ],
        compiler_params=vmem_params(),
        cost_estimate=pl.CostEstimate(flops=1, bytes_accessed=1, transcendentals=0),
        name="own_half",
    )(side, place, count, their_place, their_count, tensor, *pieces)


def add_piece(piece, tensor, gathered, own_half, total):
    def step(index, carry):
        row = STARTS[piece] + index * TILE
        position, offset = row // ROWS, pl.multiple_of(row % ROWS, TILE)
        start = pl.multiple_of(index * TILE, TILE)
        product = jnp.dot(tensor[pl.ds(start, TILE), :], gathered[position], preferred_element_type=jnp.float32)
        total[...] += lax.dot_general(
            own_half[position, pl.ds(offset, TILE), :],
            product.astype(jnp.bfloat16),
            (((1,), (1,)), ((), ())),
            preferred_element_type=jnp.float32,
        )
        return carry

    lax.fori_loop(0, (STARTS[piece + 1] - STARTS[piece]) // TILE, step, 0)


def pair_kernel(theirs, gathered, own_half, out, total):
    total[...] = jnp.zeros_like(total)
    add_piece(0, theirs, gathered, own_half, total)
    tile = total[0:BS, 0:BS]
    for block in range(1, TILE // BS):
        rows = slice(block * BS, (block + 1) * BS)
        tile += total[rows, rows]
    flat = jnp.concatenate([tile[: BS // 2], tile[BS // 2 :]], axis=1)
    for target in range(16):
        out[target * (BS // 2) : (target + 1) * (BS // 2), :] = flat


def pair_part(theirs, gathered, own_half):
    return pl.pallas_call(
        pair_kernel,
        in_specs=in_vmem(3),
        out_specs=in_vmem(1)[0],
        out_shape=jax.ShapeDtypeStruct((16 * BS // 2, 2 * BS), jnp.float32),
        scratch_shapes=[pltpu.VMEM((TILE, TILE), jnp.float32)],
        compiler_params=vmem_params(),
        cost_estimate=pl.CostEstimate(flops=1, bytes_accessed=1, transcendentals=0),
        name="pair_tile",
    )(theirs, gathered, own_half)


def sum_kernel(side, tiles, out):
    sums = []
    for zp in range(2):
        flat = tiles[zp * (BS // 2) : (zp + 1) * (BS // 2), :]
        for source in range(1, 8):
            start = (source * 2 + zp) * (BS // 2)
            flat = flat + tiles[start : start + BS // 2, :]
        sums.append(jnp.concatenate([flat[:, :BS], flat[:, BS:]], axis=0))
    low, high = sums
    scale = -1.0 / math.sqrt(32 * AB * NOCC)

    @pl.when(side[0] == 0)
    def _():
        out[...] = (low + high.T) * scale

    @pl.when(side[0] == 1)
    def _():
        out[...] = (high + low.T) * scale


def sum_part(side, tiles):
    return pl.pallas_call(
        sum_kernel,
        in_specs=[pl.BlockSpec(memory_space=pltpu.SMEM)] + in_vmem(1),
        out_specs=in_vmem(1)[0],
        out_shape=jax.ShapeDtypeStruct((BS, BS), jnp.float32),
        name="sum_tiles",
    )(side, tiles)


def prepare_kernel(strip, pattern, count, screen, density, out):
    keep = screen[0, strip[0]] != 0
    value = jnp.where(keep, density[...], jnp.zeros((BS, OBS), jnp.bfloat16))
    lanes = lax.broadcasted_iota(jnp.int32, (HEADER, OBS), 1)
    row = jnp.zeros((HEADER, OBS), jnp.int32)
    for position in range(4):
        for slot in range(KNZ):
            row = jnp.where(lanes == position * KNZ + slot, pattern[position, slot], row)
        row = jnp.where(lanes == 4 * KNZ + position, count[position, 0], row)
    row = row.astype(jnp.float32).astype(jnp.bfloat16)
    for copy in range(4):
        start = copy * (BS + HEADER)
        out[start : start + BS, :] = value
        out[start + BS : start + BS + HEADER, :] = row


def prepare(strip, pattern, count, screen, density):
    rows = 4 * (BS + HEADER)
    spec = pltpu.PrefetchScalarGridSpec(
        num_scalar_prefetch=4,
        grid=(1,),
        in_specs=[pl.BlockSpec((BS, OBS), lambda j, strip, *_: (0, strip[0]))],
        out_specs=pl.BlockSpec((rows, OBS), lambda j, *_: (0, 0)),
    )
    return pl.pallas_call(
        prepare_kernel,
        grid_spec=spec,
        out_shape=jax.ShapeDtypeStruct((rows, OBS), jnp.bfloat16),
        name="prepare",
    )(strip, pattern, count, screen, density)


def places(blocks):
    high, y, core = blocks // 16, (blocks // 2) % 8, blocks % 2
    return (core != lax.axis_index("c")) * PLANE + y * COLUMN + high * BS


def spread(value, axis, count):
    copies = jnp.broadcast_to(value[None], (count, *value.shape)).reshape(-1, value.shape[-1])
    return lax.all_to_all(copies, axis, 0, 0, tiled=True)


def gather_plane(column):
    plane = spread(column[:, :BS].reshape(COLUMN, OBS), "y", 8)
    strips = spread(plane, "x", 4)
    return strips, lax.ppermute(strips, "c", SWAP)


def no_plane(column):
    blank = jnp.zeros((4 * PLANE, OBS), column.dtype)
    return blank, blank


def per_device(three_center, pattern, live_count, density_factor, screen):
    side = lax.axis_index("zp")
    tensor = three_center.reshape(4 * ROWS, COLS)
    pattern, live_count = pattern.reshape(4, KNZ), live_count.reshape(4, 1)
    copies = prepare(lax.axis_index("x").reshape(1), pattern, live_count, screen, density_factor)
    column = lax.all_to_all(copies, ("zp", "zm"), 0, 0, tiled=True)
    sent = lax.dynamic_slice_in_dim(tensor, (1 - side) * (2 * ROWS), 2 * ROWS, 0)
    column, sent = lax.optimization_barrier((column, sent))
    theirs = lax.ppermute(sent, "zp", SWAP)

    column = column.reshape(4, BS + HEADER, OBS)
    partner = (1 - side) * 2 + lax.axis_index("zm")
    numbers = lax.dynamic_slice(column, (partner, BS, 0), (1, 1, OBS)).reshape(-1).astype(jnp.int32)
    split = 4 * KNZ
    where = (places(pattern.reshape(-1)), live_count.reshape(-1), places(numbers[:split]), numbers[split : split + 4])
    column, where = lax.optimization_barrier((column, where))
    pieces = lax.cond(live_count[0, 0] > 0, gather_plane, no_plane, column)
    own_half, their_gathered = own_part(
        side.reshape(1),
        *where,
        tensor.reshape(4, ROWS, COLS),
        pieces,
    )
    tiles = pair_part(theirs, their_gathered, own_half)
    tiles = lax.all_to_all(tiles, ("x", "zl", "zp"), 0, 0, tiled=True)
    return sum_part(side.reshape(1), tiles)


def solution(mesh):
    parts = Mesh(mesh.devices.reshape(4, 2, 2, 2, 8, 2), ("x", "zl", "zp", "zm", "y", "c"))
    placed = (
        P(AUX, ROW, None, None),
        P(AUX, ROW, None),
        P(AUX, ROW),
        P(ROW, None),
        P(ROW, None),
    )
    return jax.shard_map(
        per_device, mesh=parts, in_specs=placed, out_specs=P(ROW, None), check_vma=False
    )
```

```python
import math

import jax
import jax.numpy as jnp
from jax import lax
from jax.experimental import pallas as pl
from jax.experimental.pallas import tpu as pltpu
from jax.sharding import Mesh, PartitionSpec as P

BS = 64
AB = 16
KNZ = 6
OBS = 128
NOCC = 512
ROWS = AB * BS
COLS = KNZ * BS
TILE = 256
STEP = 512
AUX = ("x", "zl")
ROW = ("zp", "zm", "y", "c")
SWAP = [(0, 1), (1, 0)]
COLUMN = 4 * BS
PLANE = 8 * COLUMN
HEADER = 16
VMEM_BYTES = 40 * 2**20


def vmem_params():
    return pltpu.CompilerParams(vmem_limit_bytes=VMEM_BYTES)


def in_vmem(count):
    return [pl.BlockSpec(memory_space=pltpu.VMEM)] * count


def gather_slots(whole, gathered, place, count, position):
    for slot in range(KNZ):
        rows = pl.ds(slot * BS, BS)
        start = pl.multiple_of(place[position * KNZ + slot], BS)
        alive = slot < count[position]

        @pl.when(alive)
        def _():
            gathered[rows, :] = whole[pl.ds(start, BS), :]

        @pl.when(jnp.logical_not(alive))
        def _():
            gathered[rows, :] = jnp.zeros((BS, NOCC), jnp.bfloat16)


def load_whole(pieces, whole, sem):
    copies = []
    for core, piece in enumerate(pieces):
        for block in range(NOCC // OBS):
            rows, columns = pl.ds(core * PLANE, PLANE), pl.ds(block * OBS, OBS)
            source = piece.at[pl.ds(block * PLANE, PLANE), :]
            copy = pltpu.make_async_copy(source, whole.at[rows, columns], sem.at[core * 4 + block])
            copy.start()
            copies.append(copy)
    for copy in copies:
        copy.wait()


def transform(tensor, gathered):
    return jnp.dot(tensor, gathered, preferred_element_type=jnp.float32).astype(jnp.bfloat16)


def add_terms(total, own, theirs):
    for tile in range(own.shape[0] // TILE):
        rows = slice(tile * TILE, (tile + 1) * TILE)
        total[...] += lax.dot_general(
            own[rows], theirs[rows], (((1,), (1,)), ((), ())), preferred_element_type=jnp.float32
        )


def first_kernel(side, place, count, their_place, their_count, *refs):
    own, next_own, theirs, strips, other_strips, total, next_half, next_gathered = refs[:8]
    gathered, whole, sem = refs[8:]

    @pl.when(pl.program_id(0) == 0)
    def _():
        load_whole((strips, other_strips), whole, sem)
        for offset in range(2):
            position = side[0] * 2 + offset
            gather_slots(whole, gathered.at[offset], place, count, position)
            target = next_gathered if offset else gathered.at[2]
            gather_slots(whole, target, their_place, their_count, position)
        total[...] = jnp.zeros_like(total)

    add_terms(total, transform(own[0], gathered[0]), transform(theirs[...], gathered[2]))
    next_half[...] = transform(next_own[0], gathered[1])


def first_part(side, place, count, their_place, their_count, tensor, theirs, strips):
    fixed = lambda j, *_: (0, 0)
    spec = pltpu.PrefetchScalarGridSpec(
        num_scalar_prefetch=5,
        grid=(ROWS // STEP,),
        in_specs=[
            pl.BlockSpec((1, STEP, COLS), lambda j, side, *_: (side[0] * 2, j, 0)),
            pl.BlockSpec((1, STEP, COLS), lambda j, side, *_: (side[0] * 2 + 1, j, 0)),
            pl.BlockSpec((STEP, COLS), lambda j, *_: (j, 0)),
            pl.BlockSpec(memory_space=pl.ANY),
            pl.BlockSpec(memory_space=pl.ANY),
        ],
        out_specs=[
            pl.BlockSpec((TILE, TILE), fixed),
            pl.BlockSpec((STEP, NOCC), lambda j, *_: (j, 0)),
            pl.BlockSpec((COLS, NOCC), fixed),
        ],
        scratch_shapes=[
            pltpu.VMEM((3, COLS, NOCC), jnp.bfloat16),
            pltpu.VMEM((2 * PLANE, NOCC), jnp.bfloat16),
            pltpu.SemaphoreType.DMA((8,)),
        ],
    )
    return pl.pallas_call(
        first_kernel,
        grid_spec=spec,
        out_shape=[
            jax.ShapeDtypeStruct((TILE, TILE), jnp.float32),
            jax.ShapeDtypeStruct((ROWS, NOCC), jnp.bfloat16),
            jax.ShapeDtypeStruct((COLS, NOCC), jnp.bfloat16),
        ],
        compiler_params=vmem_params(),
        cost_estimate=pl.CostEstimate(flops=1, bytes_accessed=1, transcendentals=0),
        name="first_block",
    )(side, place, count, their_place, their_count, tensor, tensor, theirs, *strips)


def second_kernel(theirs, gathered, own_half, before, out, total):
    @pl.when(pl.program_id(0) == 0)
    def _():
        total[...] = before[...]

    add_terms(total, own_half[...], transform(theirs[...], gathered[...]))

    @pl.when(pl.program_id(0) == pl.num_programs(0) - 1)
    def _():
        tile = total[0:BS, 0:BS]
        for block in range(1, TILE // BS):
            rows = slice(block * BS, (block + 1) * BS)
            tile += total[rows, rows]
        flat = jnp.concatenate([tile[: BS // 2], tile[BS // 2 :]], axis=1)
        for target in range(16):
            out[target * (BS // 2) : (target + 1) * (BS // 2), :] = flat


def second_part(theirs, gathered, own_half, before):
    fixed = lambda j: (0, 0)
    shape = (16 * BS // 2, 2 * BS)
    return pl.pallas_call(
        second_kernel,
        grid=(ROWS // STEP,),
        in_specs=[
            pl.BlockSpec((STEP, COLS), lambda j: (j, 0)),
            pl.BlockSpec((COLS, NOCC), fixed),
            pl.BlockSpec((STEP, NOCC), lambda j: (j, 0)),
            pl.BlockSpec((TILE, TILE), fixed),
        ],
        out_specs=pl.BlockSpec(shape, fixed),
        out_shape=jax.ShapeDtypeStruct(shape, jnp.float32),
        scratch_shapes=[pltpu.VMEM((TILE, TILE), jnp.float32)],
        compiler_params=vmem_params(),
        cost_estimate=pl.CostEstimate(flops=1, bytes_accessed=1, transcendentals=0),
        name="second_block",
    )(theirs, gathered, own_half, before)


def sum_kernel(side, tiles, out):
    sums = []
    for zp in range(2):
        flat = tiles[zp * (BS // 2) : (zp + 1) * (BS // 2), :]
        for source in range(1, 8):
            start = (source * 2 + zp) * (BS // 2)
            flat = flat + tiles[start : start + BS // 2, :]
        sums.append(jnp.concatenate([flat[:, :BS], flat[:, BS:]], axis=0))
    low, high = sums
    scale = -1.0 / math.sqrt(32 * AB * NOCC)

    @pl.when(side[0] == 0)
    def _():
        out[...] = (low + high.T) * scale

    @pl.when(side[0] == 1)
    def _():
        out[...] = (high + low.T) * scale


def sum_part(side, tiles):
    return pl.pallas_call(
        sum_kernel,
        in_specs=[pl.BlockSpec(memory_space=pltpu.SMEM)] + in_vmem(1),
        out_specs=in_vmem(1)[0],
        out_shape=jax.ShapeDtypeStruct((BS, BS), jnp.float32),
        name="sum_tiles",
    )(side, tiles)


def prepare_kernel(strip, pattern, count, screen, start, density, tensor, out, first, second, sem):
    moves = []
    for index, target in enumerate((first, second)):
        source = tensor.at[pl.ds(pl.multiple_of(start[0] + index * ROWS, ROWS), ROWS), :]
        moves.append(pltpu.make_async_copy(source, target, sem.at[index]))
        moves[-1].start()
    keep = screen[0, strip[0]] != 0
    value = jnp.where(keep, density[...], jnp.zeros((BS, OBS), jnp.bfloat16))
    lanes = lax.broadcasted_iota(jnp.int32, (HEADER, OBS), 1)
    row = jnp.zeros((HEADER, OBS), jnp.int32)
    for position in range(4):
        for slot in range(KNZ):
            row = jnp.where(lanes == position * KNZ + slot, pattern[position, slot], row)
        row = jnp.where(lanes == 4 * KNZ + position, count[0, position], row)
    row = row.astype(jnp.float32).astype(jnp.bfloat16)
    for copy in range(4):
        top = copy * (BS + HEADER)
        out[top : top + BS, :] = value
        out[top + BS : top + BS + HEADER, :] = row
    for move in moves:
        move.wait()


def prepare(strip, pattern, count, screen, start, density, tensor):
    rows = 4 * (BS + HEADER)
    spec = pltpu.PrefetchScalarGridSpec(
        num_scalar_prefetch=5,
        grid=(1,),
        in_specs=[
            pl.BlockSpec((BS, OBS), lambda j, strip, *_: (0, strip[0])),
            pl.BlockSpec(memory_space=pl.ANY),
        ],
        out_specs=[
            pl.BlockSpec((rows, OBS), lambda j, *_: (0, 0)),
            pl.BlockSpec((ROWS, COLS), lambda j, *_: (0, 0)),
            pl.BlockSpec((ROWS, COLS), lambda j, *_: (0, 0)),
        ],
        scratch_shapes=[pltpu.SemaphoreType.DMA((2,))],
    )
    piece = jax.ShapeDtypeStruct((ROWS, COLS), jnp.bfloat16)
    return pl.pallas_call(
        prepare_kernel,
        grid_spec=spec,
        out_shape=[jax.ShapeDtypeStruct((rows, OBS), jnp.bfloat16), piece, piece],
        cost_estimate=pl.CostEstimate(flops=1, bytes_accessed=1, transcendentals=0),
        name="prepare",
    )(strip, pattern, count, screen, start, density, tensor)


def places(blocks):
    high, y, core = blocks // 16, (blocks // 2) % 8, blocks % 2
    return (core != lax.axis_index("c")) * PLANE + y * COLUMN + high * BS


def spread(value, axis, count):
    copies = jnp.broadcast_to(value[None], (count, *value.shape)).reshape(-1, value.shape[-1])
    return lax.all_to_all(copies, axis, 0, 0, tiled=True)


def gather_plane(column):
    plane = spread(column[:, :BS].reshape(COLUMN, OBS), "y", 8)
    strips = spread(plane, "x", 4)
    return strips, lax.ppermute(strips, "c", SWAP)


def no_plane(column):
    blank = jnp.zeros((4 * PLANE, OBS), column.dtype)
    return blank, blank


def per_device(three_center, pattern, live_count, density_factor, screen):
    side = lax.axis_index("zp")
    tensor = three_center.reshape(4 * ROWS, COLS)
    pattern, live_count = pattern.reshape(4, KNZ), live_count.reshape(1, 4)
    start = ((1 - side) * (2 * ROWS)).reshape(1)
    strip = lax.axis_index("x").reshape(1)
    copies, first, second = prepare(strip, pattern, live_count, screen, start, density_factor, tensor)
    column = lax.all_to_all(copies, ("zp", "zm"), 0, 0, tiled=True)
    second, column = lax.optimization_barrier((second, column))
    theirs = [lax.ppermute(piece, "zp", SWAP) for piece in (first, second)]

    column = column.reshape(4, BS + HEADER, OBS)
    partner = (1 - side) * 2 + lax.axis_index("zm")
    numbers = lax.dynamic_slice(column, (partner, BS, 0), (1, 1, OBS)).reshape(-1).astype(jnp.int32)
    split = 4 * KNZ
    where = (places(pattern.reshape(-1)), live_count.reshape(-1), places(numbers[:split]), numbers[split : split + 4])
    column, where = lax.optimization_barrier((column, where))
    strips = lax.cond(live_count[0, 0] > 0, gather_plane, no_plane, column)
    tensor = tensor.reshape(4, ROWS, COLS)
    total, own_half, gathered = first_part(side.reshape(1), *where, tensor, theirs[0], strips)
    tiles = second_part(theirs[1], gathered, own_half, total)
    tiles = lax.all_to_all(tiles, ("x", "zl", "zp"), 0, 0, tiled=True)
    return sum_part(side.reshape(1), tiles)


def solution(mesh):
    parts = Mesh(mesh.devices.reshape(4, 2, 2, 2, 8, 2), ("x", "zl", "zp", "zm", "y", "c"))
    placed = (
        P(AUX, ROW, None, None),
        P(AUX, ROW, None),
        P(AUX, ROW),
        P(ROW, None),
        P(ROW, None),
    )
    return jax.shard_map(
        per_device, mesh=parts, in_specs=placed, out_specs=P(ROW, None), check_vma=False
    )
```

```python
import math

import jax
import jax.numpy as jnp
from jax import lax
from jax.experimental import pallas as pl
from jax.experimental.pallas import tpu as pltpu
from jax.sharding import Mesh, PartitionSpec as P

BS = 64
AB = 16
KNZ = 6
OBS = 128
NOCC = 512
ROWS = AB * BS
COLS = KNZ * BS
TILE = 256
STEP = 1024
AUX = ("x", "zl")
ROW = ("zp", "zm", "y", "c")
SWAP = [(0, 1), (1, 0)]
COLUMN = 4 * BS
PLANE = 8 * COLUMN
HEADER = 16
VMEM_BYTES = 24 * 2**20


def vmem_params():
    return pltpu.CompilerParams(vmem_limit_bytes=VMEM_BYTES)


def in_vmem(count):
    return [pl.BlockSpec(memory_space=pltpu.VMEM)] * count


def gather_slots(strips, gathered, core, block_of, count):
    def fill(slot, own, source):
        block = block_of(slot)
        start = pl.multiple_of((block // 2) % 8 * COLUMN + block // 16 * BS, BS)

        @pl.when((slot < count) & ((block % 2 == core) == own))
        def _():
            for strip in range(NOCC // OBS):
                rows, columns = pl.ds(strip * PLANE + start, BS), slice(strip * OBS, (strip + 1) * OBS)
                gathered[slot * BS : (slot + 1) * BS, columns] = source[rows, :]

    for slot in range(KNZ):
        fill(slot, True, strips[0])
        fill(slot, False, strips[1])

        @pl.when(slot >= count)
        def _():
            gathered[slot * BS : (slot + 1) * BS, :] = jnp.zeros((BS, NOCC), jnp.bfloat16)


def transform(tensor, gathered):
    return jnp.dot(tensor, gathered, preferred_element_type=jnp.float32).astype(jnp.bfloat16)


def add_terms(total, own, theirs):
    for tile in range(own.shape[0] // TILE):
        rows = slice(tile * TILE, (tile + 1) * TILE)
        total[...] += lax.dot_general(
            own[rows], theirs[rows], (((1,), (1,)), ((), ())), preferred_element_type=jnp.float32
        )


def first_kernel(side, core, pattern, count, numbers, *refs):
    own, next_own, theirs, strips, other_strips, total, next_half, next_gathered = refs[:8]
    gathered = refs[8]

    @pl.when(pl.program_id(0) == 0)
    def _():
        pair = (strips, other_strips)
        for offset in range(2):
            position = side[0] * 2 + offset
            target = next_gathered if offset else gathered.at[2]
            gather_slots(
                pair, gathered.at[offset], core[0], lambda slot: pattern[position, slot], count[0, position]
            )
            gather_slots(
                pair, target, core[0], lambda slot: numbers[position * KNZ + slot], numbers[4 * KNZ + position]
            )
        total[...] = jnp.zeros_like(total)

    add_terms(total, transform(own[0], gathered[0]), transform(theirs[...], gathered[2]))
    next_half[...] = transform(next_own[0], gathered[1])


def first_part(side, core, pattern, count, numbers, tensor, theirs, strips):
    fixed = lambda j, *_: (0, 0)
    spec = pltpu.PrefetchScalarGridSpec(
        num_scalar_prefetch=5,
        grid=(ROWS // STEP,),
        in_specs=[
            pl.BlockSpec((1, STEP, COLS), lambda j, side, *_: (side[0] * 2, j, 0)),
            pl.BlockSpec((1, STEP, COLS), lambda j, side, *_: (side[0] * 2 + 1, j, 0)),
            pl.BlockSpec((STEP, COLS), lambda j, *_: (j, 0)),
            pl.BlockSpec(strips[0].shape, fixed),
            pl.BlockSpec(strips[1].shape, fixed),
        ],
        out_specs=[
            pl.BlockSpec((TILE, TILE), fixed),
            pl.BlockSpec((STEP, NOCC), lambda j, *_: (j, 0)),
            pl.BlockSpec((COLS, NOCC), fixed),
        ],
        scratch_shapes=[pltpu.VMEM((3, COLS, NOCC), jnp.bfloat16)],
    )
    return pl.pallas_call(
        first_kernel,
        grid_spec=spec,
        out_shape=[
            jax.ShapeDtypeStruct((TILE, TILE), jnp.float32),
            jax.ShapeDtypeStruct((ROWS, NOCC), jnp.bfloat16),
            jax.ShapeDtypeStruct((COLS, NOCC), jnp.bfloat16),
        ],
        compiler_params=vmem_params(),
        cost_estimate=pl.CostEstimate(flops=1, bytes_accessed=1, transcendentals=0),
        name="first_block",
    )(side, core, pattern, count, numbers, tensor, tensor, theirs, *strips)


def second_kernel(theirs, gathered, own_half, before, out, total):
    total[...] = before[...]
    add_terms(total, own_half[...], transform(theirs[...], gathered[...]))
    tile = total[0:BS, 0:BS]
    for block in range(1, TILE // BS):
        rows = slice(block * BS, (block + 1) * BS)
        tile += total[rows, rows]
    flat = jnp.concatenate([tile[: BS // 2], tile[BS // 2 :]], axis=1)
    for target in range(16):
        out[target * (BS // 2) : (target + 1) * (BS // 2), :] = flat


def second_part(theirs, gathered, own_half, before):
    return pl.pallas_call(
        second_kernel,
        in_specs=in_vmem(4),
        out_specs=in_vmem(1)[0],
        out_shape=jax.ShapeDtypeStruct((16 * BS // 2, 2 * BS), jnp.float32),
        scratch_shapes=[pltpu.VMEM((TILE, TILE), jnp.float32)],
        compiler_params=vmem_params(),
        cost_estimate=pl.CostEstimate(flops=1, bytes_accessed=1, transcendentals=0),
        name="second_block",
    )(theirs, gathered, own_half, before)


def sum_kernel(tiles, out):
    side = lax.axis_index("zp")
    sums = []
    for zp in range(2):
        flat = tiles[zp * (BS // 2) : (zp + 1) * (BS // 2), :]
        for source in range(1, 8):
            start = (source * 2 + zp) * (BS // 2)
            flat = flat + tiles[start : start + BS // 2, :]
        sums.append(jnp.concatenate([flat[:, :BS], flat[:, BS:]], axis=0))
    low, high = sums
    scale = -1.0 / math.sqrt(32 * AB * NOCC)

    @pl.when(side == 0)
    def _():
        out[...] = (low + high.T) * scale

    @pl.when(side == 1)
    def _():
        out[...] = (high + low.T) * scale


def sum_part(tiles):
    return pl.pallas_call(
        sum_kernel,
        in_specs=in_vmem(1),
        out_specs=in_vmem(1)[0],
        out_shape=jax.ShapeDtypeStruct((BS, BS), jnp.float32),
        name="sum_tiles",
    )(tiles)


def prepare_kernel(strip, pattern, count, screen, start, density, tensor, out, first, sem):
    source = tensor.at[pl.ds(pl.multiple_of(start[0], ROWS), ROWS), :]
    move = pltpu.make_async_copy(source, first, sem)
    move.start()
    keep = screen[0, strip[0]] != 0
    value = jnp.where(keep, density[...], jnp.zeros((BS, OBS), jnp.bfloat16))
    lanes = lax.broadcasted_iota(jnp.int32, (HEADER, OBS), 1)
    row = jnp.zeros((HEADER, OBS), jnp.int32)
    for position in range(4):
        for slot in range(KNZ):
            row = jnp.where(lanes == position * KNZ + slot, pattern[position, slot], row)
        row = jnp.where(lanes == 4 * KNZ + position, count[0, position], row)
    row = row.astype(jnp.float32).astype(jnp.bfloat16)
    for copy in range(4):
        top = copy * (BS + HEADER)
        out[top : top + BS, :] = value
        out[top + BS : top + BS + HEADER, :] = row
    move.wait()


def prepare(strip, pattern, count, screen, start, density, tensor):
    rows = 4 * (BS + HEADER)
    spec = pltpu.PrefetchScalarGridSpec(
        num_scalar_prefetch=5,
        grid=(1,),
        in_specs=[
            pl.BlockSpec((BS, OBS), lambda j, strip, *_: (0, strip[0])),
            pl.BlockSpec(memory_space=pl.ANY),
        ],
        out_specs=[
            pl.BlockSpec((rows, OBS), lambda j, *_: (0, 0)),
            pl.BlockSpec((ROWS, COLS), lambda j, *_: (0, 0)),
        ],
        scratch_shapes=[pltpu.SemaphoreType.DMA],
    )
    return pl.pallas_call(
        prepare_kernel,
        grid_spec=spec,
        out_shape=[
            jax.ShapeDtypeStruct((rows, OBS), jnp.bfloat16),
            jax.ShapeDtypeStruct((ROWS, COLS), jnp.bfloat16),
        ],
        cost_estimate=pl.CostEstimate(flops=1, bytes_accessed=1, transcendentals=0),
        name="prepare",
    )(strip, pattern, count, screen, start, density, tensor)


def cut_kernel(start, tensor, piece, sem):
    source = tensor.at[pl.ds(pl.multiple_of(start[0] + ROWS, ROWS), ROWS), :]
    move = pltpu.make_async_copy(source, piece, sem)
    move.start()
    move.wait()


def cut_second(start, tensor):
    return pl.pallas_call(
        cut_kernel,
        in_specs=[pl.BlockSpec(memory_space=pltpu.SMEM), pl.BlockSpec(memory_space=pl.ANY)],
        out_specs=in_vmem(1)[0],
        out_shape=jax.ShapeDtypeStruct((ROWS, COLS), jnp.bfloat16),
        scratch_shapes=[pltpu.SemaphoreType.DMA],
        cost_estimate=pl.CostEstimate(flops=1, bytes_accessed=1, transcendentals=0),
        name="cut_second",
    )(start, tensor)


def spread(value, axis, count):
    copies = jnp.broadcast_to(value[None], (count, *value.shape)).reshape(-1, value.shape[-1])
    return lax.all_to_all(copies, axis, 0, 0, tiled=True)


def gather_plane(column):
    plane = spread(column[:, :BS].reshape(COLUMN, OBS), "y", 8)
    strips = spread(plane, "x", 4)
    return strips, lax.ppermute(strips, "c", SWAP)


def no_plane(column):
    blank = jnp.zeros((4 * PLANE, OBS), column.dtype)
    return blank, blank


def per_device(three_center, pattern, live_count, density_factor, screen):
    side = lax.axis_index("zp")
    tensor = three_center.reshape(4 * ROWS, COLS)
    pattern, live_count = pattern.reshape(4, KNZ), live_count.reshape(1, 4)
    start = ((1 - side) * (2 * ROWS)).reshape(1)
    strip = lax.axis_index("x").reshape(1)
    copies, first = prepare(strip, pattern, live_count, screen, start, density_factor, tensor)
    column = lax.all_to_all(copies, ("zp", "zm"), 0, 0, tiled=True)
    second, column = lax.optimization_barrier((cut_second(start, tensor), column))
    theirs = [lax.ppermute(piece, "zp", SWAP) for piece in (first, second)]

    column = column.reshape(4, BS + HEADER, OBS)
    partner = (1 - side) * 2 + lax.axis_index("zm")
    numbers = lax.dynamic_slice(column, (partner, BS, 0), (1, 1, OBS)).reshape(-1).astype(jnp.int32)
    strips = lax.cond(live_count[0, 0] > 0, gather_plane, no_plane, column)
    tensor = tensor.reshape(4, ROWS, COLS)
    core = lax.axis_index("c").reshape(1)
    total, own_half, gathered = first_part(
        side.reshape(1), core, pattern, live_count, numbers, tensor, theirs[0], strips
    )
    tiles = second_part(theirs[1], gathered, own_half, total)
    tiles = lax.all_to_all(tiles, ("x", "zl", "zp"), 0, 0, tiled=True)
    return sum_part(tiles)


def solution(mesh):
    parts = Mesh(mesh.devices.reshape(4, 2, 2, 2, 8, 2), ("x", "zl", "zp", "zm", "y", "c"))
    placed = (
        P(AUX, ROW, None, None),
        P(AUX, ROW, None),
        P(AUX, ROW),
        P(ROW, None),
        P(ROW, None),
    )
    return jax.shard_map(
        per_device, mesh=parts, in_specs=placed, out_specs=P(ROW, None), check_vma=False
    )
```

```python
import math

import jax
import jax.numpy as jnp
from jax import lax
from jax.experimental import pallas as pl
from jax.experimental.pallas import tpu as pltpu
from jax.sharding import Mesh, PartitionSpec as P

BS = 64
AB = 16
KNZ = 6
OBS = 128
NOCC = 512
ROWS = AB * BS
COLS = KNZ * BS
TILE = 256
STEP = 1024
AUX = ("x", "zl")
ROW = ("zp", "zm", "y", "c")
SWAP = [(0, 1), (1, 0)]
COLUMN = 4 * BS
PLANE = 8 * COLUMN
HEADER = 16
VMEM_BYTES = 24 * 2**20


def vmem_params(size=VMEM_BYTES):
    return pltpu.CompilerParams(vmem_limit_bytes=size)


def in_vmem(count):
    return [pl.BlockSpec(memory_space=pltpu.VMEM)] * count


def gather_slots(strips, gathered, core, block_of, count):
    def fill(slot, own, source):
        block = block_of(slot)
        start = pl.multiple_of((block // 2) % 8 * COLUMN + block // 16 * BS, BS)

        @pl.when((slot < count) & ((block % 2 == core) == own))
        def _():
            for strip in range(NOCC // OBS):
                rows, columns = pl.ds(strip * PLANE + start, BS), slice(strip * OBS, (strip + 1) * OBS)
                gathered[slot * BS : (slot + 1) * BS, columns] = source[rows, :]

    for slot in range(KNZ):
        fill(slot, True, strips[0])
        fill(slot, False, strips[1])

        @pl.when(slot >= count)
        def _():
            gathered[slot * BS : (slot + 1) * BS, :] = jnp.zeros((BS, NOCC), jnp.bfloat16)


def transform(tensor, gathered):
    return jnp.dot(tensor, gathered, preferred_element_type=jnp.float32).astype(jnp.bfloat16)


def add_terms(total, own, theirs):
    for tile in range(own.shape[0] // TILE):
        rows = slice(tile * TILE, (tile + 1) * TILE)
        total[...] += lax.dot_general(
            own[rows], theirs[rows], (((1,), (1,)), ((), ())), preferred_element_type=jnp.float32
        )


def first_kernel(side, core, pattern, count, numbers, *refs):
    own, next_own, theirs, strips, other_strips, total, next_half, next_gathered = refs[:8]
    gathered = refs[8]

    @pl.when(pl.program_id(0) == 0)
    def _():
        pair = (strips, other_strips)
        for offset in range(2):
            position = side[0] * 2 + offset
            target = next_gathered if offset else gathered.at[2]
            gather_slots(
                pair, gathered.at[offset], core[0], lambda slot: pattern[position, slot], count[0, position]
            )
            gather_slots(
                pair, target, core[0], lambda slot: numbers[position * KNZ + slot], numbers[4 * KNZ + position]
            )
        total[...] = jnp.zeros_like(total)

    add_terms(total, transform(own[0], gathered[0]), transform(theirs[...], gathered[2]))
    next_half[...] = transform(next_own[0], gathered[1])


def first_part(side, core, pattern, count, numbers, tensor, theirs, strips):
    fixed = lambda j, *_: (0, 0)
    spec = pltpu.PrefetchScalarGridSpec(
        num_scalar_prefetch=5,
        grid=(ROWS // STEP,),
        in_specs=[
            pl.BlockSpec((1, STEP, COLS), lambda j, side, *_: (side[0] * 2, j, 0)),
            pl.BlockSpec((1, STEP, COLS), lambda j, side, *_: (side[0] * 2 + 1, j, 0)),
            pl.BlockSpec((STEP, COLS), lambda j, *_: (j, 0)),
            pl.BlockSpec(strips[0].shape, fixed),
            pl.BlockSpec(strips[1].shape, fixed),
        ],
        out_specs=[
            pl.BlockSpec((TILE, TILE), fixed),
            pl.BlockSpec((STEP, NOCC), lambda j, *_: (j, 0)),
            pl.BlockSpec((COLS, NOCC), fixed),
        ],
        scratch_shapes=[pltpu.VMEM((3, COLS, NOCC), jnp.bfloat16)],
    )
    return pl.pallas_call(
        first_kernel,
        grid_spec=spec,
        out_shape=[
            jax.ShapeDtypeStruct((TILE, TILE), jnp.float32),
            jax.ShapeDtypeStruct((ROWS, NOCC), jnp.bfloat16),
            jax.ShapeDtypeStruct((COLS, NOCC), jnp.bfloat16),
        ],
        compiler_params=vmem_params(),
        cost_estimate=pl.CostEstimate(flops=1, bytes_accessed=1, transcendentals=0),
        name="first_block",
    )(side, core, pattern, count, numbers, tensor, tensor, theirs, *strips)


def second_kernel(theirs, gathered, own_half, before, out, total):
    total[...] = before[...]
    add_terms(total, own_half[...], transform(theirs[...], gathered[...]))
    tile = total[0:BS, 0:BS]
    for block in range(1, TILE // BS):
        rows = slice(block * BS, (block + 1) * BS)
        tile += total[rows, rows]
    flat = jnp.concatenate([tile[: BS // 2], tile[BS // 2 :]], axis=1)
    for target in range(16):
        out[target * (BS // 2) : (target + 1) * (BS // 2), :] = flat


def second_part(theirs, gathered, own_half, before):
    return pl.pallas_call(
        second_kernel,
        in_specs=in_vmem(4),
        out_specs=in_vmem(1)[0],
        out_shape=jax.ShapeDtypeStruct((16 * BS // 2, 2 * BS), jnp.float32),
        scratch_shapes=[pltpu.VMEM((TILE, TILE), jnp.float32)],
        compiler_params=vmem_params(),
        cost_estimate=pl.CostEstimate(flops=1, bytes_accessed=1, transcendentals=0),
        name="second_block",
    )(theirs, gathered, own_half, before)


def sum_kernel(tiles, out):
    side = lax.axis_index("zp")
    sums = []
    for zp in range(2):
        flat = tiles[zp * (BS // 2) : (zp + 1) * (BS // 2), :]
        for source in range(1, 8):
            start = (source * 2 + zp) * (BS // 2)
            flat = flat + tiles[start : start + BS // 2, :]
        sums.append(jnp.concatenate([flat[:, :BS], flat[:, BS:]], axis=0))
    low, high = sums
    scale = -1.0 / math.sqrt(32 * AB * NOCC)

    @pl.when(side == 0)
    def _():
        out[...] = (low + high.T) * scale

    @pl.when(side == 1)
    def _():
        out[...] = (high + low.T) * scale


def sum_part(tiles):
    return pl.pallas_call(
        sum_kernel,
        in_specs=in_vmem(1),
        out_specs=in_vmem(1)[0],
        out_shape=jax.ShapeDtypeStruct((BS, BS), jnp.float32),
        compiler_params=vmem_params(4 * 2**20),
        name="sum_tiles",
    )(tiles)


def prepare_kernel(strip, pattern, count, screen, start, density, tensor, out, first, sem):
    source = tensor.at[pl.ds(pl.multiple_of(start[0], ROWS), ROWS), :]
    move = pltpu.make_async_copy(source, first, sem)
    move.start()
    keep = screen[0, strip[0]] != 0
    value = jnp.where(keep, density[...], jnp.zeros((BS, OBS), jnp.bfloat16))
    lanes = lax.broadcasted_iota(jnp.int32, (HEADER, OBS), 1)
    row = jnp.zeros((HEADER, OBS), jnp.int32)
    for position in range(4):
        for slot in range(KNZ):
            row = jnp.where(lanes == position * KNZ + slot, pattern[position, slot], row)
        row = jnp.where(lanes == 4 * KNZ + position, count[0, position], row)
    row = row.astype(jnp.float32).astype(jnp.bfloat16)
    for copy in range(4):
        top = copy * (BS + HEADER)
        out[top : top + BS, :] = value
        out[top + BS : top + BS + HEADER, :] = row
    move.wait()


def prepare(strip, pattern, count, screen, start, density, tensor):
    rows = 4 * (BS + HEADER)
    spec = pltpu.PrefetchScalarGridSpec(
        num_scalar_prefetch=5,
        grid=(1,),
        in_specs=[
            pl.BlockSpec((BS, OBS), lambda j, strip, *_: (0, strip[0])),
            pl.BlockSpec(memory_space=pl.ANY),
        ],
        out_specs=[
            pl.BlockSpec((rows, OBS), lambda j, *_: (0, 0)),
            pl.BlockSpec((ROWS, COLS), lambda j, *_: (0, 0)),
        ],
        scratch_shapes=[pltpu.SemaphoreType.DMA],
    )
    return pl.pallas_call(
        prepare_kernel,
        grid_spec=spec,
        out_shape=[
            jax.ShapeDtypeStruct((rows, OBS), jnp.bfloat16),
            jax.ShapeDtypeStruct((ROWS, COLS), jnp.bfloat16),
        ],
        cost_estimate=pl.CostEstimate(flops=1, bytes_accessed=1, transcendentals=0),
        name="prepare",
    )(strip, pattern, count, screen, start, density, tensor)


def cut_kernel(start, tensor, piece, sem):
    source = tensor.at[pl.ds(pl.multiple_of(start[0] + ROWS, ROWS), ROWS), :]
    move = pltpu.make_async_copy(source, piece, sem)
    move.start()
    move.wait()


def cut_second(start, tensor):
    return pl.pallas_call(
        cut_kernel,
        in_specs=[pl.BlockSpec(memory_space=pltpu.SMEM), pl.BlockSpec(memory_space=pl.ANY)],
        out_specs=in_vmem(1)[0],
        out_shape=jax.ShapeDtypeStruct((ROWS, COLS), jnp.bfloat16),
        scratch_shapes=[pltpu.SemaphoreType.DMA],
        cost_estimate=pl.CostEstimate(flops=1, bytes_accessed=1, transcendentals=0),
        name="cut_second",
    )(start, tensor)


def spread(value, axis, count):
    copies = jnp.broadcast_to(value[None], (count, *value.shape)).reshape(-1, value.shape[-1])
    return lax.all_to_all(copies, axis, 0, 0, tiled=True)


def gather_plane(column):
    plane = spread(column[:, :BS].reshape(COLUMN, OBS), "y", 8)
    strips = spread(plane, "x", 4)
    return strips, lax.ppermute(strips, "c", SWAP)


def no_plane(column):
    blank = jnp.zeros((4 * PLANE, OBS), column.dtype)
    return blank, blank


def per_device(three_center, pattern, live_count, density_factor, screen):
    side = lax.axis_index("zp")
    tensor = three_center.reshape(4 * ROWS, COLS)
    pattern, live_count = pattern.reshape(4, KNZ), live_count.reshape(1, 4)
    start = ((1 - side) * (2 * ROWS)).reshape(1)
    strip = lax.axis_index("x").reshape(1)
    copies, first = prepare(strip, pattern, live_count, screen, start, density_factor, tensor)
    column = lax.all_to_all(copies, ("zp", "zm"), 0, 0, tiled=True)
    second, column = lax.optimization_barrier((cut_second(start, tensor), column))
    theirs = [lax.ppermute(piece, "zp", SWAP) for piece in (first, second)]

    column = column.reshape(4, BS + HEADER, OBS)
    partner = (1 - side) * 2 + lax.axis_index("zm")
    numbers = lax.dynamic_slice(column, (partner, BS, 0), (1, 1, OBS)).reshape(-1).astype(jnp.int32)
    strips = lax.cond(live_count[0, 0] > 0, gather_plane, no_plane, column)
    tensor = tensor.reshape(4, ROWS, COLS)
    core = lax.axis_index("c").reshape(1)
    total, own_half, gathered = first_part(
        side.reshape(1), core, pattern, live_count, numbers, tensor, theirs[0], strips
    )
    tiles = second_part(theirs[1], gathered, own_half, total)
    tiles = lax.all_to_all(tiles, ("x", "zl", "zp"), 0, 0, tiled=True)
    return sum_part(tiles)


def solution(mesh):
    parts = Mesh(mesh.devices.reshape(4, 2, 2, 2, 8, 2), ("x", "zl", "zp", "zm", "y", "c"))
    placed = (
        P(AUX, ROW, None, None),
        P(AUX, ROW, None),
        P(AUX, ROW),
        P(ROW, None),
        P(ROW, None),
    )
    return jax.shard_map(
        per_device, mesh=parts, in_specs=placed, out_specs=P(ROW, None), check_vma=False
    )
```

```python
import math

import jax
import jax.numpy as jnp
from jax import lax
from jax.experimental import pallas as pl
from jax.experimental.pallas import tpu as pltpu
from jax.sharding import Mesh, PartitionSpec as P

BS = 64
AB = 16
KNZ = 6
OBS = 128
NOCC = 512
ROWS = AB * BS
COLS = KNZ * BS
TILE = 256
STEP = 1024
AUX = ("x", "zl")
ROW = ("zp", "zm", "y", "c")
SWAP = [(0, 1), (1, 0)]
COLUMN = 4 * BS
PLANE = 8 * COLUMN
HEADER = 16
VMEM_BYTES = 24 * 2**20


def vmem_params(size=VMEM_BYTES):
    return pltpu.CompilerParams(vmem_limit_bytes=size)


def in_vmem(count):
    return [pl.BlockSpec(memory_space=pltpu.VMEM)] * count


def gather_slots(strips, gathered, core, block_of, count):
    def fill(slot, own, source):
        block = block_of(slot)
        start = pl.multiple_of((block // 2) % 8 * COLUMN + block // 16 * BS, BS)

        @pl.when((slot < count) & ((block % 2 == core) == own))
        def _():
            for strip in range(NOCC // OBS):
                rows, columns = pl.ds(strip * PLANE + start, BS), slice(strip * OBS, (strip + 1) * OBS)
                gathered[slot * BS : (slot + 1) * BS, columns] = source[rows, :]

    for slot in range(KNZ):
        fill(slot, True, strips[0])
        fill(slot, False, strips[1])

        @pl.when(slot >= count)
        def _():
            gathered[slot * BS : (slot + 1) * BS, :] = jnp.zeros((BS, NOCC), jnp.bfloat16)


def transform(tensor, gathered):
    return jnp.dot(tensor, gathered, preferred_element_type=jnp.float32).astype(jnp.bfloat16)


def add_terms(total, own, theirs):
    for tile in range(own.shape[0] // TILE):
        rows = slice(tile * TILE, (tile + 1) * TILE)
        total[...] += lax.dot_general(
            own[rows], theirs[rows], (((1,), (1,)), ((), ())), preferred_element_type=jnp.float32
        )


def first_kernel(side, core, pattern, count, numbers, *refs):
    own, next_own, theirs, strips, other_strips, total, next_half, next_gathered = refs[:8]
    gathered = refs[8]

    @pl.when(pl.program_id(0) == 0)
    def _():
        pair = (strips, other_strips)
        for offset in range(2):
            position = side[0] * 2 + offset
            target = next_gathered if offset else gathered.at[2]
            gather_slots(
                pair, gathered.at[offset], core[0], lambda slot: pattern[position, slot], count[0, position]
            )
            gather_slots(
                pair, target, core[0], lambda slot: numbers[position * KNZ + slot], numbers[4 * KNZ + position]
            )
        total[...] = jnp.zeros_like(total)

    add_terms(total, transform(own[0], gathered[0]), transform(theirs[...], gathered[2]))
    next_half[...] = transform(next_own[0], gathered[1])


def first_part(side, core, pattern, count, numbers, tensor, theirs, strips):
    fixed = lambda j, *_: (0, 0)
    spec = pltpu.PrefetchScalarGridSpec(
        num_scalar_prefetch=5,
        grid=(ROWS // STEP,),
        in_specs=[
            pl.BlockSpec((1, STEP, COLS), lambda j, side, *_: (side[0] * 2, j, 0)),
            pl.BlockSpec((1, STEP, COLS), lambda j, side, *_: (side[0] * 2 + 1, j, 0)),
            pl.BlockSpec((STEP, COLS), lambda j, *_: (j, 0)),
            pl.BlockSpec(strips[0].shape, fixed),
            pl.BlockSpec(strips[1].shape, fixed),
        ],
        out_specs=[
            pl.BlockSpec((TILE, TILE), fixed),
            pl.BlockSpec((STEP, NOCC), lambda j, *_: (j, 0)),
            pl.BlockSpec((COLS, NOCC), fixed),
        ],
        scratch_shapes=[pltpu.VMEM((3, COLS, NOCC), jnp.bfloat16)],
    )
    return pl.pallas_call(
        first_kernel,
        grid_spec=spec,
        out_shape=[
            jax.ShapeDtypeStruct((TILE, TILE), jnp.float32),
            jax.ShapeDtypeStruct((ROWS, NOCC), jnp.bfloat16),
            jax.ShapeDtypeStruct((COLS, NOCC), jnp.bfloat16),
        ],
        compiler_params=vmem_params(),
        cost_estimate=pl.CostEstimate(flops=1, bytes_accessed=1, transcendentals=0),
        name="first_block",
    )(side, core, pattern, count, numbers, tensor, tensor, theirs, *strips)


def second_kernel(theirs, gathered, own_half, before, out, total):
    total[...] = before[...]
    add_terms(total, own_half[...], transform(theirs[...], gathered[...]))
    tile = total[0:BS, 0:BS]
    for block in range(1, TILE // BS):
        rows = slice(block * BS, (block + 1) * BS)
        tile += total[rows, rows]
    flat = jnp.concatenate([tile[: BS // 2], tile[BS // 2 :]], axis=1)
    for target in range(16):
        out[target * (BS // 2) : (target + 1) * (BS // 2), :] = flat


def second_part(theirs, gathered, own_half, before):
    return pl.pallas_call(
        second_kernel,
        in_specs=in_vmem(4),
        out_specs=in_vmem(1)[0],
        out_shape=jax.ShapeDtypeStruct((16 * BS // 2, 2 * BS), jnp.float32),
        scratch_shapes=[pltpu.VMEM((TILE, TILE), jnp.float32)],
        compiler_params=vmem_params(),
        cost_estimate=pl.CostEstimate(flops=1, bytes_accessed=1, transcendentals=0),
        name="second_block",
    )(theirs, gathered, own_half, before)


def sum_kernel(tiles, out):
    side = lax.axis_index("zp")
    sums = []
    for zp in range(2):
        flat = tiles[zp * (BS // 2) : (zp + 1) * (BS // 2), :]
        for source in range(1, 8):
            start = (source * 2 + zp) * (BS // 2)
            flat = flat + tiles[start : start + BS // 2, :]
        sums.append(jnp.concatenate([flat[:, :BS], flat[:, BS:]], axis=0))
    low, high = sums
    scale = -1.0 / math.sqrt(32 * AB * NOCC)

    @pl.when(side == 0)
    def _():
        out[...] = (low + high.T) * scale

    @pl.when(side == 1)
    def _():
        out[...] = (high + low.T) * scale


def sum_part(tiles):
    return pl.pallas_call(
        sum_kernel,
        in_specs=in_vmem(1),
        out_specs=in_vmem(1)[0],
        out_shape=jax.ShapeDtypeStruct((BS, BS), jnp.float32),
        compiler_params=vmem_params(4 * 2**20),
        name="sum_tiles",
    )(tiles)


def prepare_kernel(strip, pattern, count, screen, start, density, tensor, out, first, sem):
    move = pltpu.make_async_copy(tensor.at[pl.ds(pl.multiple_of(start[0], ROWS), ROWS), :], first, sem)
    move.start()
    keep = screen[0, strip[0]] != 0
    columns = pl.ds(pl.multiple_of(strip[0] * OBS, OBS), OBS)
    value = jnp.where(keep, density[:, columns], jnp.zeros((BS, OBS), jnp.bfloat16))
    lanes = lax.broadcasted_iota(jnp.int32, (HEADER, OBS), 1)
    row = jnp.zeros((HEADER, OBS), jnp.int32)
    for position in range(4):
        for slot in range(KNZ):
            row = jnp.where(lanes == position * KNZ + slot, pattern[position, slot], row)
        row = jnp.where(lanes == 4 * KNZ + position, count[0, position], row)
    row = row.astype(jnp.float32).astype(jnp.bfloat16)
    for copy in range(4):
        top = copy * (BS + HEADER)
        out[top : top + BS, :] = value
        out[top + BS : top + BS + HEADER, :] = row
    move.wait()


def prepare(strip, pattern, count, screen, start, density, tensor):
    return pl.pallas_call(
        prepare_kernel,
        in_specs=[pl.BlockSpec(memory_space=pltpu.SMEM)] * 5 + in_vmem(1) + [pl.BlockSpec(memory_space=pl.ANY)],
        out_specs=in_vmem(2),
        out_shape=[
            jax.ShapeDtypeStruct((4 * (BS + HEADER), OBS), jnp.bfloat16),
            jax.ShapeDtypeStruct((ROWS, COLS), jnp.bfloat16),
        ],
        scratch_shapes=[pltpu.SemaphoreType.DMA],
        cost_estimate=pl.CostEstimate(flops=1, bytes_accessed=1, transcendentals=0),
        name="prepare",
    )(strip, pattern, count, screen, start, density, tensor)


def cut_kernel(start, tensor, piece, sem):
    source = tensor.at[pl.ds(pl.multiple_of(start[0] + ROWS, ROWS), ROWS), :]
    move = pltpu.make_async_copy(source, piece, sem)
    move.start()
    move.wait()


def cut_second(start, tensor):
    return pl.pallas_call(
        cut_kernel,
        in_specs=[pl.BlockSpec(memory_space=pltpu.SMEM), pl.BlockSpec(memory_space=pl.ANY)],
        out_specs=in_vmem(1)[0],
        out_shape=jax.ShapeDtypeStruct((ROWS, COLS), jnp.bfloat16),
        scratch_shapes=[pltpu.SemaphoreType.DMA],
        cost_estimate=pl.CostEstimate(flops=1, bytes_accessed=1, transcendentals=0),
        name="cut_second",
    )(start, tensor)


def spread(value, axis, count):
    copies = jnp.broadcast_to(value[None], (count, *value.shape)).reshape(-1, value.shape[-1])
    return lax.all_to_all(copies, axis, 0, 0, tiled=True)


def gather_plane(column):
    plane = spread(column[:, :BS].reshape(COLUMN, OBS), "y", 8)
    strips = spread(plane, "x", 4)
    return strips, lax.ppermute(strips, "c", SWAP)


def no_plane(column):
    blank = jnp.zeros((4 * PLANE, OBS), column.dtype)
    return blank, blank


def per_device(three_center, pattern, live_count, density_factor, screen):
    side = lax.axis_index("zp")
    tensor = three_center.reshape(4 * ROWS, COLS)
    pattern, live_count = pattern.reshape(4, KNZ), live_count.reshape(1, 4)
    start = ((1 - side) * (2 * ROWS)).reshape(1)
    strip = lax.axis_index("x").reshape(1)
    copies, first = prepare(strip, pattern, live_count, screen, start, density_factor, tensor)
    column = lax.all_to_all(copies, ("zp", "zm"), 0, 0, tiled=True)
    second, column = lax.optimization_barrier((cut_second(start, tensor), column))
    theirs = [lax.ppermute(piece, "zp", SWAP) for piece in (first, second)]

    column = column.reshape(4, BS + HEADER, OBS)
    partner = (1 - side) * 2 + lax.axis_index("zm")
    numbers = lax.dynamic_slice(column, (partner, BS, 0), (1, 1, OBS)).reshape(-1).astype(jnp.int32)
    strips = lax.cond(live_count[0, 0] > 0, gather_plane, no_plane, column)
    tensor = tensor.reshape(4, ROWS, COLS)
    core = lax.axis_index("c").reshape(1)
    total, own_half, gathered = first_part(
        side.reshape(1), core, pattern, live_count, numbers, tensor, theirs[0], strips
    )
    tiles = second_part(theirs[1], gathered, own_half, total)
    tiles = lax.all_to_all(tiles, ("x", "zl", "zp"), 0, 0, tiled=True)
    return sum_part(tiles)


def solution(mesh):
    parts = Mesh(mesh.devices.reshape(4, 2, 2, 2, 8, 2), ("x", "zl", "zp", "zm", "y", "c"))
    placed = (
        P(AUX, ROW, None, None),
        P(AUX, ROW, None),
        P(AUX, ROW),
        P(ROW, None),
        P(ROW, None),
    )
    return jax.shard_map(
        per_device, mesh=parts, in_specs=placed, out_specs=P(ROW, None), check_vma=False
    )
```

```python
import math

import jax
import jax.numpy as jnp
from jax import lax
from jax.experimental import pallas as pl
from jax.experimental.pallas import tpu as pltpu
from jax.sharding import Mesh, PartitionSpec as P

BS = 64
AB = 16
KNZ = 6
OBS = 128
NOCC = 512
ROWS = AB * BS
COLS = KNZ * BS
TILE = 256
STEP = 1024
AUX = ("x", "zl")
ROW = ("zp", "zm", "y", "c")
SWAP = [(0, 1), (1, 0)]
COLUMN = 4 * BS
PLANE = 8 * COLUMN
HEADER = 16
VMEM_BYTES = 24 * 2**20


def vmem_params(size=VMEM_BYTES):
    return pltpu.CompilerParams(vmem_limit_bytes=size)


def in_vmem(count):
    return [pl.BlockSpec(memory_space=pltpu.VMEM)] * count


def gather_slots(strips, gathered, core, block_of, count):
    def fill(slot, own, source):
        block = block_of(slot)
        start = pl.multiple_of((block // 2) % 8 * COLUMN + block // 16 * BS, BS)

        @pl.when((slot < count) & ((block % 2 == core) == own))
        def _():
            for strip in range(NOCC // OBS):
                rows, columns = pl.ds(strip * PLANE + start, BS), slice(strip * OBS, (strip + 1) * OBS)
                gathered[slot * BS : (slot + 1) * BS, columns] = source[rows, :]

    for slot in range(KNZ):
        fill(slot, True, strips[0])
        fill(slot, False, strips[1])

        @pl.when(slot >= count)
        def _():
            gathered[slot * BS : (slot + 1) * BS, :] = jnp.zeros((BS, NOCC), jnp.bfloat16)


def transform(tensor, gathered):
    return jnp.dot(tensor, gathered, preferred_element_type=jnp.float32).astype(jnp.bfloat16)


def add_terms(total, own, theirs):
    for tile in range(own.shape[0] // TILE):
        rows = slice(tile * TILE, (tile + 1) * TILE)
        total[...] += lax.dot_general(
            own[rows], theirs[rows], (((1,), (1,)), ((), ())), preferred_element_type=jnp.float32
        )


def first_kernel(side, core, pattern, count, numbers, *refs):
    own, next_own, theirs, strips, other_strips, total, next_term, gathered = refs

    @pl.when(pl.program_id(0) == 0)
    def _():
        pair = (strips, other_strips)
        for offset in range(2):
            position = side[0] * 2 + offset
            gather_slots(
                pair, gathered.at[offset], core[0], lambda slot: pattern[position, slot], count[0, position]
            )
            gather_slots(
                pair, gathered.at[2 + offset], core[0], lambda slot: numbers[position * KNZ + slot], numbers[4 * KNZ + position]
            )
        total[...] = jnp.zeros_like(total)

    add_terms(total, transform(own[0], gathered[0]), transform(theirs[...], gathered[2]))
    half = transform(next_own[0], gathered[1])
    next_term[...] = lax.dot_general(
        half, gathered[3], (((1,), (1,)), ((), ())), preferred_element_type=jnp.float32
    ).astype(jnp.bfloat16)


def first_part(side, core, pattern, count, numbers, tensor, theirs, strips):
    fixed = lambda j, *_: (0, 0)
    spec = pltpu.PrefetchScalarGridSpec(
        num_scalar_prefetch=5,
        grid=(ROWS // STEP,),
        in_specs=[
            pl.BlockSpec((1, STEP, COLS), lambda j, side, *_: (side[0] * 2, j, 0)),
            pl.BlockSpec((1, STEP, COLS), lambda j, side, *_: (side[0] * 2 + 1, j, 0)),
            pl.BlockSpec((STEP, COLS), lambda j, *_: (j, 0)),
            pl.BlockSpec(strips[0].shape, fixed),
            pl.BlockSpec(strips[1].shape, fixed),
        ],
        out_specs=[
            pl.BlockSpec((TILE, TILE), fixed),
            pl.BlockSpec((STEP, COLS), lambda j, *_: (j, 0)),
        ],
        scratch_shapes=[pltpu.VMEM((4, COLS, NOCC), jnp.bfloat16)],
    )
    return pl.pallas_call(
        first_kernel,
        grid_spec=spec,
        out_shape=[
            jax.ShapeDtypeStruct((TILE, TILE), jnp.float32),
            jax.ShapeDtypeStruct((ROWS, COLS), jnp.bfloat16),
        ],
        compiler_params=vmem_params(),
        cost_estimate=pl.CostEstimate(flops=1, bytes_accessed=1, transcendentals=0),
        name="first_block",
    )(side, core, pattern, count, numbers, tensor, tensor, theirs, *strips)


def second_kernel(theirs, own_term, before, out, total):
    total[...] = before[...]
    add_terms(total, own_term[...], theirs[...])
    tile = total[0:BS, 0:BS]
    for block in range(1, TILE // BS):
        rows = slice(block * BS, (block + 1) * BS)
        tile += total[rows, rows]
    flat = jnp.concatenate([tile[: BS // 2], tile[BS // 2 :]], axis=1)
    for target in range(16):
        out[target * (BS // 2) : (target + 1) * (BS // 2), :] = flat


def second_part(theirs, own_term, before):
    return pl.pallas_call(
        second_kernel,
        in_specs=in_vmem(3),
        out_specs=in_vmem(1)[0],
        out_shape=jax.ShapeDtypeStruct((16 * BS // 2, 2 * BS), jnp.float32),
        scratch_shapes=[pltpu.VMEM((TILE, TILE), jnp.float32)],
        compiler_params=vmem_params(),
        cost_estimate=pl.CostEstimate(flops=1, bytes_accessed=1, transcendentals=0),
        name="second_block",
    )(theirs, own_term, before)


def sum_kernel(tiles, out):
    side = lax.axis_index("zp")
    sums = []
    for zp in range(2):
        flat = tiles[zp * (BS // 2) : (zp + 1) * (BS // 2), :]
        for source in range(1, 8):
            start = (source * 2 + zp) * (BS // 2)
            flat = flat + tiles[start : start + BS // 2, :]
        sums.append(jnp.concatenate([flat[:, :BS], flat[:, BS:]], axis=0))
    low, high = sums
    scale = -1.0 / math.sqrt(32 * AB * NOCC)

    @pl.when(side == 0)
    def _():
        out[...] = (low + high.T) * scale

    @pl.when(side == 1)
    def _():
        out[...] = (high + low.T) * scale


def sum_part(tiles):
    return pl.pallas_call(
        sum_kernel,
        in_specs=in_vmem(1),
        out_specs=in_vmem(1)[0],
        out_shape=jax.ShapeDtypeStruct((BS, BS), jnp.float32),
        compiler_params=vmem_params(4 * 2**20),
        name="sum_tiles",
    )(tiles)


def prepare_kernel(strip, pattern, count, screen, start, density, tensor, out, first, sem):
    move = pltpu.make_async_copy(tensor.at[pl.ds(pl.multiple_of(start[0], ROWS), ROWS), :], first, sem)
    move.start()
    keep = screen[0, strip[0]] != 0
    columns = pl.ds(pl.multiple_of(strip[0] * OBS, OBS), OBS)
    value = jnp.where(keep, density[:, columns], jnp.zeros((BS, OBS), jnp.bfloat16))
    lanes = lax.broadcasted_iota(jnp.int32, (HEADER, OBS), 1)
    row = jnp.zeros((HEADER, OBS), jnp.int32)
    for position in range(4):
        for slot in range(KNZ):
            row = jnp.where(lanes == position * KNZ + slot, pattern[position, slot], row)
        row = jnp.where(lanes == 4 * KNZ + position, count[0, position], row)
    row = row.astype(jnp.float32).astype(jnp.bfloat16)
    for copy in range(4):
        top = copy * (BS + HEADER)
        out[top : top + BS, :] = value
        out[top + BS : top + BS + HEADER, :] = row
    move.wait()


def prepare(strip, pattern, count, screen, start, density, tensor):
    return pl.pallas_call(
        prepare_kernel,
        in_specs=[pl.BlockSpec(memory_space=pltpu.SMEM)] * 5 + in_vmem(1) + [pl.BlockSpec(memory_space=pl.ANY)],
        out_specs=in_vmem(2),
        out_shape=[
            jax.ShapeDtypeStruct((4 * (BS + HEADER), OBS), jnp.bfloat16),
            jax.ShapeDtypeStruct((ROWS, COLS), jnp.bfloat16),
        ],
        scratch_shapes=[pltpu.SemaphoreType.DMA],
        cost_estimate=pl.CostEstimate(flops=1, bytes_accessed=1, transcendentals=0),
        name="prepare",
    )(strip, pattern, count, screen, start, density, tensor)


def cut_kernel(start, tensor, piece, sem):
    source = tensor.at[pl.ds(pl.multiple_of(start[0] + ROWS, ROWS), ROWS), :]
    move = pltpu.make_async_copy(source, piece, sem)
    move.start()
    move.wait()


def cut_second(start, tensor):
    return pl.pallas_call(
        cut_kernel,
        in_specs=[pl.BlockSpec(memory_space=pltpu.SMEM), pl.BlockSpec(memory_space=pl.ANY)],
        out_specs=in_vmem(1)[0],
        out_shape=jax.ShapeDtypeStruct((ROWS, COLS), jnp.bfloat16),
        scratch_shapes=[pltpu.SemaphoreType.DMA],
        cost_estimate=pl.CostEstimate(flops=1, bytes_accessed=1, transcendentals=0),
        name="cut_second",
    )(start, tensor)


def spread(value, axis, count):
    copies = jnp.broadcast_to(value[None], (count, *value.shape)).reshape(-1, value.shape[-1])
    return lax.all_to_all(copies, axis, 0, 0, tiled=True)


def gather_plane(column):
    plane = spread(column[:, :BS].reshape(COLUMN, OBS), "y", 8)
    strips = spread(plane, "x", 4)
    return strips, lax.ppermute(strips, "c", SWAP)


def no_plane(column):
    blank = jnp.zeros((4 * PLANE, OBS), column.dtype)
    return blank, blank


def per_device(three_center, pattern, live_count, density_factor, screen):
    side = lax.axis_index("zp")
    tensor = three_center.reshape(4 * ROWS, COLS)
    pattern, live_count = pattern.reshape(4, KNZ), live_count.reshape(1, 4)
    start = ((1 - side) * (2 * ROWS)).reshape(1)
    strip = lax.axis_index("x").reshape(1)
    copies, first = prepare(strip, pattern, live_count, screen, start, density_factor, tensor)
    column = lax.all_to_all(copies, ("zp", "zm"), 0, 0, tiled=True)
    second, column = lax.optimization_barrier((cut_second(start, tensor), column))
    theirs = [lax.ppermute(piece, "zp", SWAP) for piece in (first, second)]

    column = column.reshape(4, BS + HEADER, OBS)
    partner = (1 - side) * 2 + lax.axis_index("zm")
    numbers = lax.dynamic_slice(column, (partner, BS, 0), (1, 1, OBS)).reshape(-1).astype(jnp.int32)
    strips = lax.cond(live_count[0, 0] > 0, gather_plane, no_plane, column)
    tensor = tensor.reshape(4, ROWS, COLS)
    core = lax.axis_index("c").reshape(1)
    total, own_term = first_part(
        side.reshape(1), core, pattern, live_count, numbers, tensor, theirs[0], strips
    )
    tiles = second_part(theirs[1], own_term, total)
    tiles = lax.all_to_all(tiles, ("x", "zl", "zp"), 0, 0, tiled=True)
    return sum_part(tiles)


def solution(mesh):
    parts = Mesh(mesh.devices.reshape(4, 2, 2, 2, 8, 2), ("x", "zl", "zp", "zm", "y", "c"))
    placed = (
        P(AUX, ROW, None, None),
        P(AUX, ROW, None),
        P(AUX, ROW),
        P(ROW, None),
        P(ROW, None),
    )
    return jax.shard_map(
        per_device, mesh=parts, in_specs=placed, out_specs=P(ROW, None), check_vma=False
    )
```

```python
import math

import jax
import jax.numpy as jnp
from jax import lax
from jax.experimental import pallas as pl
from jax.experimental.pallas import tpu as pltpu
from jax.sharding import Mesh, PartitionSpec as P

BS = 64
AB = 16
KNZ = 6
OBS = 128
NOCC = 512
ROWS = AB * BS
COLS = KNZ * BS
TILE = 256
STEP = 1024
AUX = ("x", "zl")
ROW = ("zp", "zm", "y", "c")
SWAP = [(0, 1), (1, 0)]
COLUMN = 4 * BS
PLANE = 8 * COLUMN
HEADER = 16
VMEM_BYTES = 24 * 2**20


def vmem_params(size=VMEM_BYTES):
    return pltpu.CompilerParams(vmem_limit_bytes=size)


def in_vmem(count):
    return [pl.BlockSpec(memory_space=pltpu.VMEM)] * count


def gather_slots(strips, gathered, core, block_of, count):
    def fill(slot, own, source):
        block = block_of(slot)
        start = pl.multiple_of((block // 2) % 8 * COLUMN + block // 16 * BS, BS)

        @pl.when((slot < count) & ((block % 2 == core) == own))
        def _():
            for strip in range(NOCC // OBS):
                rows, columns = pl.ds(strip * PLANE + start, BS), slice(strip * OBS, (strip + 1) * OBS)
                gathered[slot * BS : (slot + 1) * BS, columns] = source[rows, :]

    for slot in range(KNZ):
        fill(slot, True, strips[0])
        fill(slot, False, strips[1])

        @pl.when(slot >= count)
        def _():
            gathered[slot * BS : (slot + 1) * BS, :] = jnp.zeros((BS, NOCC), jnp.bfloat16)


def transform(tensor, gathered):
    return jnp.dot(tensor, gathered, preferred_element_type=jnp.float32).astype(jnp.bfloat16)


def add_terms(total, own, theirs):
    for tile in range(own.shape[0] // TILE):
        rows = slice(tile * TILE, (tile + 1) * TILE)
        total[...] += lax.dot_general(
            own[rows], theirs[rows], (((1,), (1,)), ((), ())), preferred_element_type=jnp.float32
        )


def first_kernel(side, core, pattern, count, numbers, *refs):
    own, next_own, theirs, strips, other_strips, total, next_term, gathered = refs

    @pl.when(pl.program_id(0) == 0)
    def _():
        pair = (strips, other_strips)
        for offset in range(2):
            position = side[0] * 2 + offset
            gather_slots(
                pair, gathered.at[offset], core[0], lambda slot: pattern[position, slot], count[0, position]
            )
            gather_slots(
                pair, gathered.at[2 + offset], core[0], lambda slot: numbers[position * KNZ + slot], numbers[4 * KNZ + position]
            )
        total[...] = jnp.zeros_like(total)

    add_terms(total, transform(own[0], gathered[0]), transform(theirs[...], gathered[2]))
    half = transform(next_own[0], gathered[1])
    next_term[...] = lax.dot_general(
        half, gathered[3], (((1,), (1,)), ((), ())), preferred_element_type=jnp.float32
    ).astype(jnp.bfloat16)


def first_part(side, core, pattern, count, numbers, tensor, theirs, strips):
    fixed = lambda j, *_: (0, 0)
    spec = pltpu.PrefetchScalarGridSpec(
        num_scalar_prefetch=5,
        grid=(ROWS // STEP,),
        in_specs=[
            pl.BlockSpec((1, STEP, COLS), lambda j, side, *_: (side[0] * 2, j, 0)),
            pl.BlockSpec((1, STEP, COLS), lambda j, side, *_: (side[0] * 2 + 1, j, 0)),
            pl.BlockSpec((STEP, COLS), lambda j, *_: (j, 0)),
            pl.BlockSpec(strips[0].shape, fixed),
            pl.BlockSpec(strips[1].shape, fixed),
        ],
        out_specs=[
            pl.BlockSpec((TILE, TILE), fixed),
            pl.BlockSpec((STEP, COLS), lambda j, *_: (j, 0)),
        ],
        scratch_shapes=[pltpu.VMEM((4, COLS, NOCC), jnp.bfloat16)],
    )
    return pl.pallas_call(
        first_kernel,
        grid_spec=spec,
        out_shape=[
            jax.ShapeDtypeStruct((TILE, TILE), jnp.float32),
            jax.ShapeDtypeStruct((ROWS, COLS), jnp.bfloat16),
        ],
        compiler_params=vmem_params(),
        cost_estimate=pl.CostEstimate(flops=1, bytes_accessed=1, transcendentals=0),
        name="first_block",
    )(side, core, pattern, count, numbers, tensor, tensor, theirs, *strips)


def second_kernel(theirs, own_term, before, out, total):
    total[...] = before[...]
    add_terms(total, own_term[...], theirs[...])
    tile = total[0:BS, 0:BS]
    for block in range(1, TILE // BS):
        rows = slice(block * BS, (block + 1) * BS)
        tile += total[rows, rows]
    flat = jnp.concatenate([tile[: BS // 2], tile[BS // 2 :]], axis=1)
    for target in range(16):
        out[target * (BS // 2) : (target + 1) * (BS // 2), :] = flat.astype(out.dtype)


def second_part(theirs, own_term, before):
    return pl.pallas_call(
        second_kernel,
        in_specs=in_vmem(3),
        out_specs=in_vmem(1)[0],
        out_shape=jax.ShapeDtypeStruct((16 * BS // 2, 2 * BS), jnp.bfloat16),
        scratch_shapes=[pltpu.VMEM((TILE, TILE), jnp.float32)],
        compiler_params=vmem_params(),
        cost_estimate=pl.CostEstimate(flops=1, bytes_accessed=1, transcendentals=0),
        name="second_block",
    )(theirs, own_term, before)


def sum_kernel(tiles, out):
    side = lax.axis_index("zp")
    sums = []
    for zp in range(2):
        flat = tiles[zp * (BS // 2) : (zp + 1) * (BS // 2), :].astype(jnp.float32)
        for source in range(1, 8):
            start = (source * 2 + zp) * (BS // 2)
            flat = flat + tiles[start : start + BS // 2, :].astype(jnp.float32)
        sums.append(jnp.concatenate([flat[:, :BS], flat[:, BS:]], axis=0))
    low, high = sums
    scale = -1.0 / math.sqrt(32 * AB * NOCC)

    @pl.when(side == 0)
    def _():
        out[...] = (low + high.T) * scale

    @pl.when(side == 1)
    def _():
        out[...] = (high + low.T) * scale


def sum_part(tiles):
    return pl.pallas_call(
        sum_kernel,
        in_specs=in_vmem(1),
        out_specs=in_vmem(1)[0],
        out_shape=jax.ShapeDtypeStruct((BS, BS), jnp.float32),
        compiler_params=vmem_params(4 * 2**20),
        name="sum_tiles",
    )(tiles)


def prepare_kernel(strip, pattern, count, screen, start, density, tensor, out, first, sem):
    move = pltpu.make_async_copy(tensor.at[pl.ds(pl.multiple_of(start[0], ROWS), ROWS), :], first, sem)
    move.start()
    keep = screen[0, strip[0]] != 0
    columns = pl.ds(pl.multiple_of(strip[0] * OBS, OBS), OBS)
    value = jnp.where(keep, density[:, columns], jnp.zeros((BS, OBS), jnp.bfloat16))
    lanes = lax.broadcasted_iota(jnp.int32, (HEADER, OBS), 1)
    row = jnp.zeros((HEADER, OBS), jnp.int32)
    for position in range(4):
        for slot in range(KNZ):
            row = jnp.where(lanes == position * KNZ + slot, pattern[position, slot], row)
        row = jnp.where(lanes == 4 * KNZ + position, count[0, position], row)
    row = row.astype(jnp.float32).astype(jnp.bfloat16)
    for copy in range(4):
        top = copy * (BS + HEADER)
        out[top : top + BS, :] = value
        out[top + BS : top + BS + HEADER, :] = row
    move.wait()


def prepare(strip, pattern, count, screen, start, density, tensor):
    return pl.pallas_call(
        prepare_kernel,
        in_specs=[pl.BlockSpec(memory_space=pltpu.SMEM)] * 5 + in_vmem(1) + [pl.BlockSpec(memory_space=pl.ANY)],
        out_specs=in_vmem(2),
        out_shape=[
            jax.ShapeDtypeStruct((4 * (BS + HEADER), OBS), jnp.bfloat16),
            jax.ShapeDtypeStruct((ROWS, COLS), jnp.bfloat16),
        ],
        scratch_shapes=[pltpu.SemaphoreType.DMA],
        cost_estimate=pl.CostEstimate(flops=1, bytes_accessed=1, transcendentals=0),
        name="prepare",
    )(strip, pattern, count, screen, start, density, tensor)


def cut_kernel(start, tensor, piece, sem):
    source = tensor.at[pl.ds(pl.multiple_of(start[0] + ROWS, ROWS), ROWS), :]
    move = pltpu.make_async_copy(source, piece, sem)
    move.start()
    move.wait()


def cut_second(start, tensor):
    return pl.pallas_call(
        cut_kernel,
        in_specs=[pl.BlockSpec(memory_space=pltpu.SMEM), pl.BlockSpec(memory_space=pl.ANY)],
        out_specs=in_vmem(1)[0],
        out_shape=jax.ShapeDtypeStruct((ROWS, COLS), jnp.bfloat16),
        scratch_shapes=[pltpu.SemaphoreType.DMA],
        cost_estimate=pl.CostEstimate(flops=1, bytes_accessed=1, transcendentals=0),
        name="cut_second",
    )(start, tensor)


def spread(value, axis, count):
    copies = jnp.broadcast_to(value[None], (count, *value.shape)).reshape(-1, value.shape[-1])
    return lax.all_to_all(copies, axis, 0, 0, tiled=True)


def gather_plane(column):
    plane = spread(column[:, :BS].reshape(COLUMN, OBS), "y", 8)
    strips = spread(plane, "x", 4)
    return strips, lax.ppermute(strips, "c", SWAP)


def no_plane(column):
    blank = jnp.zeros((4 * PLANE, OBS), column.dtype)
    return blank, blank


def per_device(three_center, pattern, live_count, density_factor, screen):
    side = lax.axis_index("zp")
    tensor = three_center.reshape(4 * ROWS, COLS)
    pattern, live_count = pattern.reshape(4, KNZ), live_count.reshape(1, 4)
    start = ((1 - side) * (2 * ROWS)).reshape(1)
    strip = lax.axis_index("x").reshape(1)
    copies, first = prepare(strip, pattern, live_count, screen, start, density_factor, tensor)
    column = lax.all_to_all(copies, ("zp", "zm"), 0, 0, tiled=True)
    second, column = lax.optimization_barrier((cut_second(start, tensor), column))
    theirs = [lax.ppermute(piece, "zp", SWAP) for piece in (first, second)]

    column = column.reshape(4, BS + HEADER, OBS)
    partner = (1 - side) * 2 + lax.axis_index("zm")
    numbers = lax.dynamic_slice(column, (partner, BS, 0), (1, 1, OBS)).reshape(-1).astype(jnp.int32)
    strips = lax.cond(live_count[0, 0] > 0, gather_plane, no_plane, column)
    tensor = tensor.reshape(4, ROWS, COLS)
    core = lax.axis_index("c").reshape(1)
    total, own_term = first_part(
        side.reshape(1), core, pattern, live_count, numbers, tensor, theirs[0], strips
    )
    tiles = second_part(theirs[1], own_term, total)
    tiles = lax.all_to_all(tiles, ("x", "zl", "zp"), 0, 0, tiled=True)
    return sum_part(tiles)


def solution(mesh):
    parts = Mesh(mesh.devices.reshape(4, 2, 2, 2, 8, 2), ("x", "zl", "zp", "zm", "y", "c"))
    placed = (
        P(AUX, ROW, None, None),
        P(AUX, ROW, None),
        P(AUX, ROW),
        P(ROW, None),
        P(ROW, None),
    )
    return jax.shard_map(
        per_device, mesh=parts, in_specs=placed, out_specs=P(ROW, None), check_vma=False
    )
```

```python
import math

import jax
import jax.numpy as jnp
from jax import lax
from jax.experimental import pallas as pl
from jax.experimental.pallas import tpu as pltpu
from jax.sharding import Mesh, PartitionSpec as P

BS = 64
AB = 16
KNZ = 6
OBS = 128
NOCC = 512
ROWS = AB * BS
COLS = KNZ * BS
TILE = 256
AUX = ("x", "zl")
ROW = ("zp", "zm", "y", "c")
SWAP = [(0, 1), (1, 0)]
COLUMN = 4 * BS
PLANE = 8 * COLUMN
HEADER = 16
VMEM_BYTES = 24 * 2**20


def vmem_params(size=VMEM_BYTES):
    return pltpu.CompilerParams(vmem_limit_bytes=size)


def in_vmem(count):
    return [pl.BlockSpec(memory_space=pltpu.VMEM)] * count


def gather_slots(strips, gathered, core, block_of, count):
    def fill(slot, own, source):
        block = block_of(slot)
        start = pl.multiple_of((block // 2) % 8 * COLUMN + block // 16 * BS, BS)

        @pl.when((slot < count) & ((block % 2 == core) == own))
        def _():
            for strip in range(NOCC // OBS):
                rows, columns = pl.ds(strip * PLANE + start, BS), slice(strip * OBS, (strip + 1) * OBS)
                gathered[slot * BS : (slot + 1) * BS, columns] = source[rows, :]

    for slot in range(KNZ):
        fill(slot, True, strips[0])
        fill(slot, False, strips[1])

        @pl.when(slot >= count)
        def _():
            gathered[slot * BS : (slot + 1) * BS, :] = jnp.zeros((BS, NOCC), jnp.bfloat16)


def transform(tensor, gathered):
    return jnp.dot(tensor, gathered, preferred_element_type=jnp.float32).astype(jnp.bfloat16)


def add_terms(total, own, theirs):
    for tile in range(own.shape[0] // TILE):
        rows = slice(tile * TILE, (tile + 1) * TILE)
        total[...] += lax.dot_general(
            own[rows], theirs[rows], (((1,), (1,)), ((), ())), preferred_element_type=jnp.float32
        )


def first_kernel(side, core, pattern, count, numbers, tensor, theirs, strips, other_strips, total, next_term, *scratch):
    own, gathered, sem = scratch

    def own_copy(offset):
        rows = pl.ds(pl.multiple_of((side[0] * 2 + offset) * ROWS, ROWS), ROWS)
        return pltpu.make_async_copy(tensor.at[rows, :], own.at[offset], sem.at[offset])

    for offset in range(2):
        own_copy(offset).start()
    pair = (strips, other_strips)
    for offset in range(2):
        position = side[0] * 2 + offset
        gather_slots(pair, gathered.at[offset], core[0], lambda slot: pattern[position, slot], count[0, position])
        gather_slots(
            pair,
            gathered.at[2 + offset],
            core[0],
            lambda slot: numbers[position * KNZ + slot],
            numbers[4 * KNZ + position],
        )
    total[...] = jnp.zeros_like(total)
    own_copy(0).wait()
    add_terms(total, transform(own[0], gathered[0]), transform(theirs[...], gathered[2]))
    own_copy(1).wait()
    half = transform(own[1], gathered[1])
    next_term[...] = lax.dot_general(
        half, gathered[3], (((1,), (1,)), ((), ())), preferred_element_type=jnp.float32
    ).astype(jnp.bfloat16)


def first_part(side, core, pattern, count, numbers, tensor, theirs, strips):
    return pl.pallas_call(
        first_kernel,
        in_specs=[pl.BlockSpec(memory_space=pltpu.SMEM)] * 5 + [pl.BlockSpec(memory_space=pl.ANY)] + in_vmem(3),
        out_specs=in_vmem(2),
        out_shape=[
            jax.ShapeDtypeStruct((TILE, TILE), jnp.float32),
            jax.ShapeDtypeStruct((ROWS, COLS), jnp.bfloat16),
        ],
        scratch_shapes=[
            pltpu.VMEM((2, ROWS, COLS), jnp.bfloat16),
            pltpu.VMEM((4, COLS, NOCC), jnp.bfloat16),
            pltpu.SemaphoreType.DMA((2,)),
        ],
        compiler_params=vmem_params(),
        cost_estimate=pl.CostEstimate(flops=1, bytes_accessed=1, transcendentals=0),
        name="first_block",
    )(side, core, pattern, count, numbers, tensor, theirs, *strips)


def second_kernel(theirs, own_term, before, out, total):
    total[...] = before[...]
    add_terms(total, own_term[...], theirs[...])
    tile = total[0:BS, 0:BS]
    for block in range(1, TILE // BS):
        rows = slice(block * BS, (block + 1) * BS)
        tile += total[rows, rows]
    flat = jnp.concatenate([tile[: BS // 2], tile[BS // 2 :]], axis=1)
    for target in range(16):
        out[target * (BS // 2) : (target + 1) * (BS // 2), :] = flat.astype(out.dtype)


def second_part(theirs, own_term, before):
    return pl.pallas_call(
        second_kernel,
        in_specs=in_vmem(3),
        out_specs=in_vmem(1)[0],
        out_shape=jax.ShapeDtypeStruct((16 * BS // 2, 2 * BS), jnp.bfloat16),
        scratch_shapes=[pltpu.VMEM((TILE, TILE), jnp.float32)],
        compiler_params=vmem_params(),
        cost_estimate=pl.CostEstimate(flops=1, bytes_accessed=1, transcendentals=0),
        name="second_block",
    )(theirs, own_term, before)


def sum_kernel(tiles, out):
    side = lax.axis_index("zp")
    sums = []
    for zp in range(2):
        flat = tiles[zp * (BS // 2) : (zp + 1) * (BS // 2), :].astype(jnp.float32)
        for source in range(1, 8):
            start = (source * 2 + zp) * (BS // 2)
            flat = flat + tiles[start : start + BS // 2, :].astype(jnp.float32)
        sums.append(jnp.concatenate([flat[:, :BS], flat[:, BS:]], axis=0))
    low, high = sums
    scale = -1.0 / math.sqrt(32 * AB * NOCC)

    @pl.when(side == 0)
    def _():
        out[...] = (low + high.T) * scale

    @pl.when(side == 1)
    def _():
        out[...] = (high + low.T) * scale


def sum_part(tiles):
    return pl.pallas_call(
        sum_kernel,
        in_specs=in_vmem(1),
        out_specs=in_vmem(1)[0],
        out_shape=jax.ShapeDtypeStruct((BS, BS), jnp.float32),
        compiler_params=vmem_params(4 * 2**20),
        name="sum_tiles",
    )(tiles)


def prepare_kernel(strip, pattern, count, screen, start, density, tensor, out, first, sem):
    move = pltpu.make_async_copy(tensor.at[pl.ds(pl.multiple_of(start[0], ROWS), ROWS), :], first, sem)
    move.start()
    keep = screen[0, strip[0]] != 0
    columns = pl.ds(pl.multiple_of(strip[0] * OBS, OBS), OBS)
    value = jnp.where(keep, density[:, columns], jnp.zeros((BS, OBS), jnp.bfloat16))
    lanes = lax.broadcasted_iota(jnp.int32, (HEADER, OBS), 1)
    row = jnp.zeros((HEADER, OBS), jnp.int32)
    for position in range(4):
        for slot in range(KNZ):
            row = jnp.where(lanes == position * KNZ + slot, pattern[position, slot], row)
        row = jnp.where(lanes == 4 * KNZ + position, count[0, position], row)
    row = row.astype(jnp.float32).astype(jnp.bfloat16)
    for copy in range(4):
        top = copy * (BS + HEADER)
        out[top : top + BS, :] = value
        out[top + BS : top + BS + HEADER, :] = row
    move.wait()


def prepare(strip, pattern, count, screen, start, density, tensor):
    return pl.pallas_call(
        prepare_kernel,
        in_specs=[pl.BlockSpec(memory_space=pltpu.SMEM)] * 5 + in_vmem(1) + [pl.BlockSpec(memory_space=pl.ANY)],
        out_specs=in_vmem(2),
        out_shape=[
            jax.ShapeDtypeStruct((4 * (BS + HEADER), OBS), jnp.bfloat16),
            jax.ShapeDtypeStruct((ROWS, COLS), jnp.bfloat16),
        ],
        scratch_shapes=[pltpu.SemaphoreType.DMA],
        cost_estimate=pl.CostEstimate(flops=1, bytes_accessed=1, transcendentals=0),
        name="prepare",
    )(strip, pattern, count, screen, start, density, tensor)


def cut_kernel(start, tensor, piece, sem):
    source = tensor.at[pl.ds(pl.multiple_of(start[0] + ROWS, ROWS), ROWS), :]
    move = pltpu.make_async_copy(source, piece, sem)
    move.start()
    move.wait()


def cut_second(start, tensor):
    return pl.pallas_call(
        cut_kernel,
        in_specs=[pl.BlockSpec(memory_space=pltpu.SMEM), pl.BlockSpec(memory_space=pl.ANY)],
        out_specs=in_vmem(1)[0],
        out_shape=jax.ShapeDtypeStruct((ROWS, COLS), jnp.bfloat16),
        scratch_shapes=[pltpu.SemaphoreType.DMA],
        cost_estimate=pl.CostEstimate(flops=1, bytes_accessed=1, transcendentals=0),
        name="cut_second",
    )(start, tensor)


def spread(value, axis, count):
    copies = jnp.broadcast_to(value[None], (count, *value.shape)).reshape(-1, value.shape[-1])
    return lax.all_to_all(copies, axis, 0, 0, tiled=True)


def gather_plane(column):
    plane = spread(column[:, :BS].reshape(COLUMN, OBS), "y", 8)
    strips = spread(plane, "x", 4)
    return strips, lax.ppermute(strips, "c", SWAP)


def no_plane(column):
    blank = jnp.zeros((4 * PLANE, OBS), column.dtype)
    return blank, blank


def per_device(three_center, pattern, live_count, density_factor, screen):
    side = lax.axis_index("zp")
    tensor = three_center.reshape(4 * ROWS, COLS)
    pattern, live_count = pattern.reshape(4, KNZ), live_count.reshape(1, 4)
    start = ((1 - side) * (2 * ROWS)).reshape(1)
    strip = lax.axis_index("x").reshape(1)
    copies, first = prepare(strip, pattern, live_count, screen, start, density_factor, tensor)
    column = lax.all_to_all(copies, ("zp", "zm"), 0, 0, tiled=True)
    second, column = lax.optimization_barrier((cut_second(start, tensor), column))
    theirs = [lax.ppermute(piece, "zp", SWAP) for piece in (first, second)]

    column = column.reshape(4, BS + HEADER, OBS)
    partner = (1 - side) * 2 + lax.axis_index("zm")
    numbers = lax.dynamic_slice(column, (partner, BS, 0), (1, 1, OBS)).reshape(-1).astype(jnp.int32)
    strips = lax.cond(live_count[0, 0] > 0, gather_plane, no_plane, column)
    core = lax.axis_index("c").reshape(1)
    total, own_term = first_part(
        side.reshape(1), core, pattern, live_count, numbers, tensor, theirs[0], strips
    )
    tiles = second_part(theirs[1], own_term, total)
    tiles = lax.all_to_all(tiles, ("x", "zl", "zp"), 0, 0, tiled=True)
    return sum_part(tiles)


def solution(mesh):
    parts = Mesh(mesh.devices.reshape(4, 2, 2, 2, 8, 2), ("x", "zl", "zp", "zm", "y", "c"))
    placed = (
        P(AUX, ROW, None, None),
        P(AUX, ROW, None),
        P(AUX, ROW),
        P(ROW, None),
        P(ROW, None),
    )
    return jax.shard_map(
        per_device, mesh=parts, in_specs=placed, out_specs=P(ROW, None), check_vma=False
    )
```

```python
import math

import jax
import jax.numpy as jnp
from jax import lax
from jax.experimental import pallas as pl
from jax.experimental.pallas import tpu as pltpu
from jax.sharding import Mesh, PartitionSpec as P

BS = 64
AB = 16
KNZ = 6
OBS = 128
NOCC = 512
ROWS = AB * BS
COLS = KNZ * BS
TILE = 256
STEP = 1024
AUX = ("x", "zl")
ROW = ("zp", "zm", "y", "c")
SWAP = [(0, 1), (1, 0)]
COLUMN = 4 * BS
PLANE = 8 * COLUMN
HEADER = 16
VMEM_BYTES = 24 * 2**20


def vmem_params(size=VMEM_BYTES):
    return pltpu.CompilerParams(vmem_limit_bytes=size)


def in_vmem(count):
    return [pl.BlockSpec(memory_space=pltpu.VMEM)] * count


def gather_slots(strips, gathered, core, block_of, count):
    def fill(slot, own, source):
        block = block_of(slot)
        start = pl.multiple_of((block // 2) % 8 * COLUMN + block // 16 * BS, BS)

        @pl.when((slot < count) & ((block % 2 == core) == own))
        def _():
            for strip in range(NOCC // OBS):
                rows, columns = pl.ds(strip * PLANE + start, BS), slice(strip * OBS, (strip + 1) * OBS)
                gathered[slot * BS : (slot + 1) * BS, columns] = source[rows, :]

    for slot in range(KNZ):
        fill(slot, True, strips[0])
        fill(slot, False, strips[1])

        @pl.when(slot >= count)
        def _():
            gathered[slot * BS : (slot + 1) * BS, :] = jnp.zeros((BS, NOCC), jnp.bfloat16)


def transform(tensor, gathered):
    return jnp.dot(tensor, gathered, preferred_element_type=jnp.float32).astype(jnp.bfloat16)


def add_terms(total, own, theirs):
    for tile in range(own.shape[0] // TILE):
        rows = slice(tile * TILE, (tile + 1) * TILE)
        total[...] += lax.dot_general(
            own[rows], theirs[rows], (((1,), (1,)), ((), ())), preferred_element_type=jnp.float32
        )


def first_kernel(side, core, pattern, count, numbers, *refs):
    own, next_own, theirs, strips, other_strips, total, next_term, gathered = refs

    @pl.when(pl.program_id(0) == 0)
    def _():
        pair = (strips, other_strips)
        for offset in range(2):
            position = side[0] * 2 + offset
            gather_slots(
                pair, gathered.at[offset], core[0], lambda slot: pattern[position, slot], count[0, position]
            )
            gather_slots(
                pair, gathered.at[2 + offset], core[0], lambda slot: numbers[position * KNZ + slot], numbers[4 * KNZ + position]
            )
        total[...] = jnp.zeros_like(total)

    add_terms(total, transform(own[0], gathered[0]), transform(theirs[...], gathered[2]))
    half = transform(next_own[0], gathered[1])
    next_term[...] = lax.dot_general(
        half, gathered[3], (((1,), (1,)), ((), ())), preferred_element_type=jnp.float32
    ).astype(jnp.bfloat16)


def first_part(side, core, pattern, count, numbers, tensor, theirs, strips):
    fixed = lambda j, *_: (0, 0)
    spec = pltpu.PrefetchScalarGridSpec(
        num_scalar_prefetch=5,
        grid=(ROWS // STEP,),
        in_specs=[
            pl.BlockSpec((1, STEP, COLS), lambda j, side, *_: (side[0] * 2, j, 0)),
            pl.BlockSpec((1, STEP, COLS), lambda j, side, *_: (side[0] * 2 + 1, j, 0)),
            pl.BlockSpec((STEP, COLS), lambda j, *_: (j, 0)),
            pl.BlockSpec(strips[0].shape, fixed),
            pl.BlockSpec(strips[1].shape, fixed),
        ],
        out_specs=[
            pl.BlockSpec((TILE, TILE), fixed),
            pl.BlockSpec((STEP, COLS), lambda j, *_: (j, 0)),
        ],
        scratch_shapes=[pltpu.VMEM((4, COLS, NOCC), jnp.bfloat16)],
    )
    return pl.pallas_call(
        first_kernel,
        grid_spec=spec,
        out_shape=[
            jax.ShapeDtypeStruct((TILE, TILE), jnp.float32),
            jax.ShapeDtypeStruct((ROWS, COLS), jnp.bfloat16),
        ],
        compiler_params=vmem_params(),
        cost_estimate=pl.CostEstimate(flops=1, bytes_accessed=1, transcendentals=0),
        name="first_block",
    )(side, core, pattern, count, numbers, tensor, tensor, theirs, *strips)


def second_kernel(theirs, own_term, before, out, total):
    total[...] = before[...]
    add_terms(total, own_term[...], theirs[...])
    tile = total[0:BS, 0:BS]
    for block in range(1, TILE // BS):
        rows = slice(block * BS, (block + 1) * BS)
        tile += total[rows, rows]
    flat = jnp.concatenate([tile[: BS // 2], tile[BS // 2 :]], axis=1)
    for target in range(16):
        out[target * (BS // 2) : (target + 1) * (BS // 2), :] = flat.astype(out.dtype)


def second_part(theirs, own_term, before):
    return pl.pallas_call(
        second_kernel,
        in_specs=in_vmem(3),
        out_specs=in_vmem(1)[0],
        out_shape=jax.ShapeDtypeStruct((16 * BS // 2, 2 * BS), jnp.bfloat16),
        scratch_shapes=[pltpu.VMEM((TILE, TILE), jnp.float32)],
        compiler_params=vmem_params(6 * 2**20),
        cost_estimate=pl.CostEstimate(flops=1, bytes_accessed=1, transcendentals=0),
        name="second_block",
    )(theirs, own_term, before)


def sum_kernel(tiles, out):
    side = lax.axis_index("zp")
    sums = []
    for zp in range(2):
        flat = tiles[zp * (BS // 2) : (zp + 1) * (BS // 2), :].astype(jnp.float32)
        for source in range(1, 8):
            start = (source * 2 + zp) * (BS // 2)
            flat = flat + tiles[start : start + BS // 2, :].astype(jnp.float32)
        sums.append(jnp.concatenate([flat[:, :BS], flat[:, BS:]], axis=0))
    low, high = sums
    scale = -1.0 / math.sqrt(32 * AB * NOCC)

    @pl.when(side == 0)
    def _():
        out[...] = (low + high.T) * scale

    @pl.when(side == 1)
    def _():
        out[...] = (high + low.T) * scale


def sum_part(tiles):
    return pl.pallas_call(
        sum_kernel,
        in_specs=in_vmem(1),
        out_specs=in_vmem(1)[0],
        out_shape=jax.ShapeDtypeStruct((BS, BS), jnp.float32),
        compiler_params=vmem_params(4 * 2**20),
        name="sum_tiles",
    )(tiles)


def prepare_kernel(strip, pattern, count, screen, start, density, tensor, out, first, sem):
    move = pltpu.make_async_copy(tensor.at[pl.ds(pl.multiple_of(start[0], ROWS), ROWS), :], first, sem)
    move.start()
    keep = screen[0, strip[0]] != 0
    columns = pl.ds(pl.multiple_of(strip[0] * OBS, OBS), OBS)
    value = jnp.where(keep, density[:, columns], jnp.zeros((BS, OBS), jnp.bfloat16))
    lanes = lax.broadcasted_iota(jnp.int32, (HEADER, OBS), 1)
    row = jnp.zeros((HEADER, OBS), jnp.int32)
    for position in range(4):
        for slot in range(KNZ):
            row = jnp.where(lanes == position * KNZ + slot, pattern[position, slot], row)
        row = jnp.where(lanes == 4 * KNZ + position, count[0, position], row)
    row = row.astype(jnp.float32).astype(jnp.bfloat16)
    for copy in range(4):
        top = copy * (BS + HEADER)
        out[top : top + BS, :] = value
        out[top + BS : top + BS + HEADER, :] = row
    move.wait()


def prepare(strip, pattern, count, screen, start, density, tensor):
    return pl.pallas_call(
        prepare_kernel,
        in_specs=[pl.BlockSpec(memory_space=pltpu.SMEM)] * 5 + in_vmem(1) + [pl.BlockSpec(memory_space=pl.ANY)],
        out_specs=in_vmem(2),
        out_shape=[
            jax.ShapeDtypeStruct((4 * (BS + HEADER), OBS), jnp.bfloat16),
            jax.ShapeDtypeStruct((ROWS, COLS), jnp.bfloat16),
        ],
        scratch_shapes=[pltpu.SemaphoreType.DMA],
        cost_estimate=pl.CostEstimate(flops=1, bytes_accessed=1, transcendentals=0),
        name="prepare",
    )(strip, pattern, count, screen, start, density, tensor)


def cut_kernel(start, tensor, piece, sem):
    source = tensor.at[pl.ds(pl.multiple_of(start[0] + ROWS, ROWS), ROWS), :]
    move = pltpu.make_async_copy(source, piece, sem)
    move.start()
    move.wait()


def cut_second(start, tensor):
    return pl.pallas_call(
        cut_kernel,
        in_specs=[pl.BlockSpec(memory_space=pltpu.SMEM), pl.BlockSpec(memory_space=pl.ANY)],
        out_specs=in_vmem(1)[0],
        out_shape=jax.ShapeDtypeStruct((ROWS, COLS), jnp.bfloat16),
        scratch_shapes=[pltpu.SemaphoreType.DMA],
        cost_estimate=pl.CostEstimate(flops=1, bytes_accessed=1, transcendentals=0),
        name="cut_second",
    )(start, tensor)


def spread(value, axis, count):
    copies = jnp.broadcast_to(value[None], (count, *value.shape)).reshape(-1, value.shape[-1])
    return lax.all_to_all(copies, axis, 0, 0, tiled=True)


def gather_plane(column):
    plane = spread(column[:, :BS].reshape(COLUMN, OBS), "y", 8)
    strips = spread(plane, "x", 4)
    return strips, lax.ppermute(strips, "c", SWAP)


def no_plane(column):
    blank = jnp.zeros((4 * PLANE, OBS), column.dtype)
    return blank, blank


def per_device(three_center, pattern, live_count, density_factor, screen):
    side = lax.axis_index("zp")
    tensor = three_center.reshape(4 * ROWS, COLS)
    pattern, live_count = pattern.reshape(4, KNZ), live_count.reshape(1, 4)
    start = ((1 - side) * (2 * ROWS)).reshape(1)
    strip = lax.axis_index("x").reshape(1)
    copies, first = prepare(strip, pattern, live_count, screen, start, density_factor, tensor)
    column = lax.all_to_all(copies, ("zp", "zm"), 0, 0, tiled=True)
    second, column = lax.optimization_barrier((cut_second(start, tensor), column))
    theirs = [lax.ppermute(piece, "zp", SWAP) for piece in (first, second)]

    column = column.reshape(4, BS + HEADER, OBS)
    partner = (1 - side) * 2 + lax.axis_index("zm")
    numbers = lax.dynamic_slice(column, (partner, BS, 0), (1, 1, OBS)).reshape(-1).astype(jnp.int32)
    strips = lax.cond(live_count[0, 0] > 0, gather_plane, no_plane, column)
    tensor = tensor.reshape(4, ROWS, COLS)
    core = lax.axis_index("c").reshape(1)
    total, own_term = first_part(
        side.reshape(1), core, pattern, live_count, numbers, tensor, theirs[0], strips
    )
    tiles = second_part(theirs[1], own_term, total)
    tiles = lax.all_to_all(tiles, ("x", "zl", "zp"), 0, 0, tiled=True)
    return sum_part(tiles)


def solution(mesh):
    parts = Mesh(mesh.devices.reshape(4, 2, 2, 2, 8, 2), ("x", "zl", "zp", "zm", "y", "c"))
    placed = (
        P(AUX, ROW, None, None),
        P(AUX, ROW, None),
        P(AUX, ROW),
        P(ROW, None),
        P(ROW, None),
    )
    return jax.shard_map(
        per_device, mesh=parts, in_specs=placed, out_specs=P(ROW, None), check_vma=False
    )
```
